128 devices in a mesh: section: 4 (over z_hi, core), expert: 32 (over z_lo, y, x).
Axes of the slice: x: 4, y: 4, z: 4 (z_hi: 2, z_lo: 2; z = z_hi * 2 + z_lo), core: 2. Of those that a mesh axis runs over, the one named last changes fastest.
Arguments:
- fwd_tokens: bfloat16 [4, 2560, 3584], P('section', 'expert'), may hold values from -6 to 6
- fwd_routes: int32 [4, 2560, 8], P('section', 'expert'), may hold values from 0 to 31, all different within a row; in each aligned block of 80 rows (0 to 79, 80 to 159, ..., all dimensions but the last counted through in order) at most 21 rows name the same one
- fwd_gates: float32 [4, 2560, 8], P('section', 'expert'), may hold values from 0.05 to 1
- bwd_grads: bfloat16 [4, 2560, 3584], P('section', 'expert'), may hold values from -6 to 6
- bwd_routes: int32 [4, 2560, 8], P('section', 'expert'), may hold values from 0 to 31, all different within a row; in each aligned block of 80 rows (0 to 79, 80 to 159, ..., all dimensions but the last counted through in order) at most 21 rows name the same one
- bwd_gates: float32 [4, 2560, 8], P('section', 'expert'), may hold values from 0.05 to 1
- saved_gate: bfloat16 [4, 2560, 8, 1024], P('section', 'expert'), may hold values from -6 to 6
- saved_up: bfloat16 [4, 2560, 8, 1024], P('section', 'expert'), may hold values from -6 to 6
- w_gate: bfloat16 [4, 32, 3584, 1024], P('section', 'expert'), may hold values from -0.09375 to 0.09375
- w_up: bfloat16 [4, 32, 3584, 1024], P('section', 'expert'), may hold values from -0.09375 to 0.09375
- w_down: bfloat16 [4, 32, 1024, 3584], P('section', 'expert'), may hold values from -0.1875 to 0.1875
Outputs:
- next_inputs: bfloat16 [4, 2560, 3584], P('section', 'expert')
- prev_grads: bfloat16 [4, 2560, 3584], P('section', 'expert')
The draws below stay inside these ranges and needn't reach their ends.
Inputs may be any that keep to these rules, and one draw needn't show every extreme that they name: `fwd_routes`: each token names 8 different experts. In the rows of one device (80 aligned tokens of one section) no expert is named by more than 21 tokens. `bwd_routes`: as for fwd_routes.
All inputs are finite; a program needn't handle non-finite values.
Results may differ from the reference program's by a relative error of at most 0.0065.
Values may be sent and summed in bfloat16 or wider, within the bound.
A program may use at most 192 MiB of HBM per device.

```python
import math
import jax
import jax.numpy as jnp
import numpy as np
from jax import lax

D = 3584
H = 1024
TOPK = 8
TOK_DEV = 80
EXPERTS = 32
TOKENS = 2560
CAP = 21
N_SECTION = 4


def level_of(own_key, dims, shards, least, high):
    def one(position, parts):
        steps = jax.random.uniform(jax.random.fold_in(jax.random.fold_in(own_key, 6), position), (parts,), jnp.float32, least / len(shards), high / len(shards))
        return jnp.repeat(jnp.exp(steps), dims[position] // parts).reshape((-1,) + (1,) * (len(dims) - position - 1))

    loudness = one(*shards[0])
    for cut in shards[1:]:
        loudness = loudness * one(*cut)
    return loudness


def routed_block(rng, own, number, rows, amount, top, most, skew):
    order = jax.random.permutation(rng, amount)
    packed, ordinary = portions_of(amount, rows * top, most, skew, True), portions_of(amount, rows * top, most, skew, False)
    places = jnp.arange(amount)

    def named(lengths, rotation):
        used = int((lengths > 0).sum())
        fixed = max(1, used // 4)
        moved = fixed + (places - fixed + rotation * (used - fixed)) % max(1, amount - fixed)
        return jnp.zeros((amount,), jnp.int32).at[order[jnp.where(places < fixed, places, moved)]].set(jnp.asarray(lengths, jnp.int32))

    lengths = jnp.where(number % 4 == 0, named(packed, number // 4), named(ordinary, number - number // 4 - 1))
    mixed = jax.random.permutation(jax.random.fold_in(own, 3), amount)
    source_of, receiver = mixed[0:amount // 2 * 2:2], mixed[1:amount // 2 * 2:2]
    margin = jnp.minimum(lengths[source_of] - 1, most - lengths[receiver]) // 2
    margin = jnp.where((source_of == order[0]) | (receiver == order[0]) | (lengths[receiver] == 0), 0, jnp.maximum(margin, 0))
    moved = jax.random.randint(jax.random.fold_in(own, 4), (amount // 2,), 0, 1 << 20) % (margin + 1)
    lengths = lengths.at[source_of].add(-moved).at[receiver].add(moved)
    items = jnp.searchsorted(jnp.cumsum(lengths), jnp.arange(rows * top), side="right").astype(jnp.int32)
    table = items.reshape(top, rows).T
    table = table[jax.random.permutation(jax.random.fold_in(own, 1), rows)]
    rotation = jax.random.randint(jax.random.fold_in(own, 2), (rows, 1), 0, top)
    return jnp.take_along_axis(table, (jnp.arange(top)[None, :] + rotation) % top, axis=1)


def portions_of(count, total, limit, lean, full):
    weights = [(1 << 20) // math.isqrt(rank ** lean) + 1 for rank in range(1, count + 1)]
    largest = limit if full else min(limit, max(-(-total // count), total * weights[0] // sum(weights)))
    least = 1 if total - largest >= count - 1 else 0
    given, surplus = [largest] + [least] * (count - 1), total - largest - least * (count - 1)
    while surplus > 0:
        movable = [i for i in range(1, count) if given[i] < largest] or [i for i in range(1, count) if given[i] < limit]
        mass, remaining = sum([weights[i] for i in movable]), surplus
        for i in movable:
            extra = min(limit - given[i], max(1, remaining * weights[i] // mass), surplus)
            given[i] = given[i] + extra
            surplus = surplus - extra
    return np.array(given)


def normal_values(own_key, extent, width, limit, cuts=(), kind=jnp.bfloat16):
    values = jax.random.normal(own_key, extent, jnp.float32) * width
    if len(cuts) > 0:
        values = level_of(own_key, extent, cuts, -0.22, 0.18) * values
    return jnp.clip(values, min=-limit, max=limit).astype(kind)


def setup_inputs(seed: int = 0) -> dict:
    streams_of = jax.random.split(jax.random.key(seed), 12)
    fwd_tokens = normal_values(streams_of[0], (N_SECTION, TOKENS, D), 1.0, 6.0, ((0, 4), (1, 32)))
    fwd_routes_keys = jax.random.split(jax.random.fold_in(streams_of[1], 1), N_SECTION * TOKENS // TOK_DEV)
    fwd_routes_turns = jax.random.permutation(jax.random.fold_in(streams_of[1], 3), N_SECTION * TOKENS // TOK_DEV)
    fwd_routes = jax.vmap(lambda own, number: routed_block(jax.random.fold_in(streams_of[1], 2), own, number, TOK_DEV, EXPERTS, TOPK, CAP, 2))(fwd_routes_keys, fwd_routes_turns).reshape((N_SECTION, TOKENS, TOPK))
    fwd_gates = jnp.clip(jnp.exp(math.log(1.0) - 2.9957323 * jax.random.uniform(streams_of[2], (N_SECTION, TOKENS, TOPK), jnp.float32) ** level_of(streams_of[2], (N_SECTION, TOKENS, TOPK), ((0, 4), (1, 32)), -0.2, 0.2)), 0.05, 1.0)
    bwd_grads = normal_values(streams_of[3], (N_SECTION, TOKENS, D), 1.0, 6.0, ((0, 4), (1, 32)))
    bwd_routes_keys = jax.random.split(jax.random.fold_in(streams_of[4], 1), N_SECTION * TOKENS // TOK_DEV)
    bwd_routes_turns = jax.random.permutation(jax.random.fold_in(streams_of[4], 3), N_SECTION * TOKENS // TOK_DEV)
    bwd_routes = jax.vmap(lambda own, number: routed_block(jax.random.fold_in(streams_of[4], 2), own, number, TOK_DEV, EXPERTS, TOPK, CAP, 2))(bwd_routes_keys, bwd_routes_turns).reshape((N_SECTION, TOKENS, TOPK))
    bwd_gates = jnp.clip(jnp.exp(math.log(1.0) - 2.9957323 * jax.random.uniform(streams_of[5], (N_SECTION, TOKENS, TOPK), jnp.float32) ** level_of(streams_of[5], (N_SECTION, TOKENS, TOPK), ((0, 4), (1, 32)), -0.2, 0.2)), 0.05, 1.0)
    saved_gate = normal_values(streams_of[6], (N_SECTION, TOKENS, TOPK, H), 1.0, 6.0, ((0, 4), (1, 32)))
    saved_up = normal_values(streams_of[7], (N_SECTION, TOKENS, TOPK, H), 1.0, 6.0, ((0, 4), (1, 32)))
    w_gate = normal_values(streams_of[8], (N_SECTION, EXPERTS, D, H), D ** -0.5, 0.09375, ((0, 4), (1, 32)))
    w_up = normal_values(streams_of[9], (N_SECTION, EXPERTS, D, H), D ** -0.5, 0.09375, ((0, 4), (1, 32)))
    w_down = normal_values(streams_of[10], (N_SECTION, EXPERTS, H, D), H ** -0.5, 0.1875, ((0, 4), (1, 32)))
    return {"fwd_tokens": fwd_tokens, "fwd_routes": fwd_routes, "fwd_gates": fwd_gates, "bwd_grads": bwd_grads, "bwd_routes": bwd_routes, "bwd_gates": bwd_gates, "saved_gate": saved_gate, "saved_up": saved_up, "w_gate": w_gate, "w_up": w_up, "w_down": w_down}


def slot_index(routes):
    onehot = (routes[:, :, None] == jnp.arange(EXPERTS, dtype=jnp.int32)[None, None, :]).astype(jnp.int32)
    counts = jnp.sum(onehot, axis=1).reshape(TOKENS // TOK_DEV, TOK_DEV, EXPERTS)
    before = (jnp.cumsum(counts, axis=1) - counts).reshape(TOKENS, EXPERTS)
    within = jnp.sum(onehot * before[:, None, :], axis=2)
    blocks = (jnp.arange(TOKENS, dtype=jnp.int32) // TOK_DEV)[:, None]
    return (blocks * CAP + within).astype(jnp.int32)


def expert_forward(inputs, gate_mat, up_mat, down_mat):
    gate_pre = jnp.dot(inputs, gate_mat, preferred_element_type=jnp.float32)
    up_pre = jnp.dot(inputs, up_mat, preferred_element_type=jnp.float32)
    hidden = (jax.nn.silu(gate_pre) * up_pre).astype(jnp.bfloat16)
    return jnp.dot(hidden, down_mat, preferred_element_type=jnp.float32).astype(jnp.bfloat16)


def expert_backward(scaled, gate_pre, up_pre, gate_mat, up_mat, down_mat):
    numbers = (((1,), (1,)), ((), ()))
    hidden_grad = lax.dot_general(scaled, down_mat, numbers, preferred_element_type=jnp.float32)
    gate_val = gate_pre.astype(jnp.float32)
    up_val = up_pre.astype(jnp.float32)
    sigmoid_a = jax.nn.sigmoid(gate_val)
    gate_grad = (hidden_grad * up_val * sigmoid_a * (1.0 + gate_val * (1.0 - sigmoid_a))).astype(jnp.bfloat16)
    up_grad = (hidden_grad * gate_val * sigmoid_a).astype(jnp.bfloat16)
    total = lax.dot_general(gate_grad, gate_mat, numbers, preferred_element_type=jnp.float32)
    total = total + lax.dot_general(up_grad, up_mat, numbers, preferred_element_type=jnp.float32)
    return total.astype(jnp.bfloat16)


def one_section(pieces):
    (fwd_tokens, fwd_routes, fwd_gates, bwd_grads, bwd_routes, bwd_gates,
     saved_gate, saved_up, w_gate, w_up, w_down) = pieces
    buffer_rows = (TOKENS // TOK_DEV) * CAP
    where_fwd = slot_index(fwd_routes)
    spread = jnp.broadcast_to(fwd_tokens[:, None, :], (TOKENS, TOPK, D))
    buffer = jnp.zeros((EXPERTS, buffer_rows, D), jnp.bfloat16).at[fwd_routes, where_fwd].set(spread)
    outputs = lax.map(lambda item: expert_forward(*item), (buffer, w_gate, w_up, w_down))
    picked = outputs[fwd_routes, where_fwd].astype(jnp.float32)
    fwd_out = jnp.sum(fwd_gates[:, :, None] * picked, axis=1).astype(jnp.bfloat16)

    where_bwd = slot_index(bwd_routes)
    scaled = (bwd_gates[:, :, None] * bwd_grads[:, None, :].astype(jnp.float32)).astype(jnp.bfloat16)
    grad_buffer = jnp.zeros((EXPERTS, buffer_rows, D), jnp.bfloat16).at[bwd_routes, where_bwd].set(scaled)
    gate_buffer = jnp.zeros((EXPERTS, buffer_rows, H), jnp.bfloat16).at[bwd_routes, where_bwd].set(saved_gate)
    up_buffer = jnp.zeros((EXPERTS, buffer_rows, H), jnp.bfloat16).at[bwd_routes, where_bwd].set(saved_up)
    row_grads = lax.map(lambda item: expert_backward(*item),
                        (grad_buffer, gate_buffer, up_buffer, w_gate, w_up, w_down))
    bwd_out = jnp.sum(row_grads[bwd_routes, where_bwd].astype(jnp.float32), axis=1).astype(jnp.bfloat16)
    return fwd_out, bwd_out


def reference(fwd_tokens, fwd_routes, fwd_gates, bwd_grads, bwd_routes, bwd_gates, saved_gate, saved_up, w_gate, w_up, w_down):
    fwd_out, bwd_out = lax.map(one_section, (fwd_tokens, fwd_routes, fwd_gates, bwd_grads, bwd_routes, bwd_gates,
                                           saved_gate, saved_up, w_gate, w_up, w_down))
    return jnp.roll(fwd_out, 1, axis=0), jnp.roll(bwd_out, -1, axis=0)
```

```python
import functools

import jax
import jax.numpy as jnp
import numpy as np
from jax import lax
from jax.experimental import pallas as pl
from jax.experimental.pallas import tpu as pltpu
from jax.sharding import PartitionSpec as P

MESH = pl.DeviceIdType.MESH
F32 = jnp.float32
BF16 = jnp.bfloat16

RING = 4
CAP = 21
TOK = 80
GROUP = RING * CAP
EXTRA = GROUP - TOK
MAIN = RING * TOK
ROWS = RING * GROUP
TAIL = ROWS - MAIN
LANES = 128
N_SEMS = 132
N_LOCAL = 24


def row_of(block, place):
    return block * TOK + place if place < TOK else MAIN + block * EXTRA + place - TOK


def swap_matrix():
    m = np.zeros((ROWS, ROWS), np.float32)
    for q in range(RING):
        for t in range(RING):
            for i in range(CAP):
                m[row_of(t, q * CAP + i), row_of(q, t * CAP + i)] = 1
    return m


def fold_matrix():
    m = np.zeros((4 * TAIL, 4 * TAIL), np.float32)
    for a in range(4):
        for b in range(4):
            for j in range(4):
                m[b * 16 + a * 4 + j, a * 16 + b * 4 + j] = 1
    return m


def dot(a, b):
    return jnp.dot(a, b, preferred_element_type=F32)


def dot_t(a, b):
    return lax.dot_general(a, b, (((1,), (1,)), ((), ())), preferred_element_type=F32)


def aligned(i, size):
    return pl.ds(pl.multiple_of(i * size, size), size)


def kernel(
    tok_hbm,
    grd_hbm,
    sg_hbm,
    su_hbm,
    wg_hbm,
    wu_hbm,
    wd_hbm,
    meta,
    spos,
    fold,
    swap,
    out_f,
    out_b,
    g_fo, g_fp, g_bo, g_bp,
    pk_fo, pk_fp, pk_bo, pk_bp,
    x_f, x_b,
    es, er, ys, yr,
    ra, rb, rc, rd, zr,
    mo, mz, mp,
    spk_o, spk_p, sg_o, sg_p, sz, sx,
    spe, sge, sze, s2e, sxe,
    hb, oh, wa, wd_t,
    send, recv, local, wsem,
):
    e = lax.axis_index("expert")
    sec = lax.axis_index("section")
    n_sec = lax.axis_size("section")
    z, y, x = e // 16, lax.rem(e // 4, 4), lax.rem(e, 4)
    me = {"y": y, "x": x}
    width = tok_hbm.shape[1]
    inner = wg_hbm.shape[1]
    half = width // 2
    F, B, O, Q = 0, 1, 0, 1
    G = ((g_fo, g_fp), (g_bo, g_bp))
    PK = ((pk_fo, pk_fp), (pk_bo, pk_bp))
    X = (x_f, x_b)
    AG_AXIS = ("y", "x")
    UNI_AXIS = ("x", "y")

    def at(axis, c):
        if axis == "y":
            return (sec, z * 16 + c * 4 + x)
        return (sec, z * 16 + y * 4 + c)

    def peer(axis, k):
        return at(axis, lax.rem(me[axis] + k, RING))

    partner = (sec, (1 - z) * 16 + y * 4 + x)
    next_sec = (lax.rem(sec + 1, n_sec), e)
    prev_sec = (lax.rem(sec + n_sec - 1, n_sec), e)

    used = [0, 0]

    def remote(src, dst, device):
        i = used[0]
        used[0] += 1
        cp = pltpu.make_async_remote_copy(
            src_ref=src, dst_ref=dst, send_sem=send.at[i], recv_sem=recv.at[i],
            device_id=device, device_id_type=MESH,
        )
        cp.start()
        return cp

    def here(src, dst):
        i = used[1]
        used[1] += 1
        cp = pltpu.make_async_copy(src, dst, local.at[i])
        cp.start()
        return cp

    def wait_recv(cps):
        for cp in cps:
            cp.wait_recv()

    def wait_send(cps):
        for cp in cps:
            cp.wait_send()

    def wa_pair(j, slot):
        cols = pl.ds(pl.multiple_of(j * LANES, LANES), LANES)
        return (
            pltpu.make_async_copy(wg_hbm.at[:, cols], wa.at[slot, :, 0:LANES], wsem.at[0, slot]),
            pltpu.make_async_copy(wu_hbm.at[:, cols], wa.at[slot, :, LANES : 2 * LANES], wsem.at[1, slot]),
        )

    def wa_down(j, slot):
        cols = pl.ds(pl.multiple_of(j * 256, 256), 256)
        return (pltpu.make_async_copy(wd_hbm.at[:, cols], wa.at[slot, 0:inner, :], wsem.at[0, slot]),)

    def wd_rows(j, slot):
        rows = aligned(j, 256)
        return (pltpu.make_async_copy(wd_hbm.at[rows, :], wd_t.at[slot], wsem.at[2, slot]),)

    def wd_pair(j, slot):
        rows = aligned(j, 256)
        return (
            pltpu.make_async_copy(wg_hbm.at[rows, :], wd_t.at[slot, :, 0:inner], wsem.at[2, slot]),
            pltpu.make_async_copy(wu_hbm.at[rows, :], wd_t.at[slot, :, inner : 2 * inner], wsem.at[3, slot]),
        )

    def begin(tiles):
        for cp in tiles(0, 0):
            cp.start()

    def stream(n, tiles, work):
        def step(j, carry):
            slot = lax.rem(j, 2)

            @pl.when(j + 1 < n)
            def _():
                for cp in tiles(j + 1, 1 - slot):
                    cp.start()

            for cp in tiles(j, slot):
                cp.wait()
            work(j, slot)
            return carry

        lax.fori_loop(0, n, step, 0)

    def fold_out(src, row0, dst):
        w4 = src.shape[1] // 4
        a = jnp.concatenate([src[row0 : row0 + TAIL, c * w4 : (c + 1) * w4] for c in range(4)], axis=0)
        dst[...] = dot(fold[...], a).astype(BF16)

    def fold_in(src, dst, row0):
        w4 = dst.shape[1] // 4
        a = dot(fold[...], src[...]).astype(BF16)
        for c in range(4):
            dst[row0 : row0 + TAIL, c * w4 : (c + 1) * w4] = a[c * TAIL : (c + 1) * TAIL, :]

    def exchange(axis, src, src_off, src_extra, dst, dst_off, dst_extra):
        m = me[axis]
        cps = []
        for k in (2, 1, 3):
            c = lax.rem(m + k, RING)
            cps.append(remote(
                src.at[pl.ds(pl.multiple_of(src_off + c * TOK, 16), TOK), :],
                dst.at[pl.ds(pl.multiple_of(dst_off + m * TOK, 16), TOK), :],
                at(axis, c)))
            cps.append(remote(src_extra.at[aligned(c, TAIL), :], dst_extra.at[aligned(m, TAIL), :], at(axis, c)))
        own = here(
            src.at[pl.ds(pl.multiple_of(src_off + m * TOK, 16), TOK), :],
            dst.at[pl.ds(pl.multiple_of(dst_off + m * TOK, 16), TOK), :])
        dst_extra[aligned(m, TAIL), :] = src_extra[aligned(m, TAIL), :]
        return cps, own

    def slot_of(ref, c, cols=None):
        rows = pl.ds(pl.multiple_of(c * TOK, 16), TOK)
        return ref.at[rows, :] if cols is None else ref.at[rows, cols]

    LO, HI = pl.ds(0, half), pl.ds(half, half)

    def gather_begin(axis, ref):
        m = me[axis]
        return [remote(slot_of(ref, m), slot_of(ref, m), peer(axis, 1)),
                remote(slot_of(ref, m), slot_of(ref, m), peer(axis, 3))]

    def gather_relay(axis, ref, first):
        m = me[axis]
        before, after = lax.rem(m + 3, RING), lax.rem(m + 1, RING)
        first[0].wait_recv()
        a = remote(slot_of(ref, before, LO), slot_of(ref, before, LO), peer(axis, 1))
        first[1].wait_recv()
        b = remote(slot_of(ref, after, HI), slot_of(ref, after, HI), peer(axis, 3))
        return [a, b]

    def pack(f, g):
        wide = lax.broadcasted_iota(jnp.int32, (TOK, LANES), 0).astype(F32)
        tail = lax.broadcasted_iota(jnp.int32, (TAIL, LANES), 0)
        tail_place = (TOK + lax.rem(tail, EXTRA)).astype(F32)
        tail_block = tail // EXTRA
        metas = (mo, mp)[g]
        for q in range(RING):
            s = metas[f, q].astype(F32)
            s = jnp.where(s >= 0, s + q * CAP, -1.0)
            cols = slice(q * LANES, (q + 1) * LANES)
            chosen = jnp.zeros((TAIL, LANES), F32)
            for t in range(RING):
                row = s[t : t + 1, :]
                oh[t * TOK : (t + 1) * TOK, cols] = jnp.where(wide == row, 1.0, 0.0).astype(BF16)
                chosen = jnp.where(tail_block == t, row, chosen)
            oh[MAIN:ROWS, cols] = jnp.where(chosen == tail_place, 1.0, 0.0).astype(BF16)

        def cols_step(j, carry):
            cols = aligned(j, 512)
            acc = dot(oh[:, 0:TOK], G[f][g][0:TOK, cols])
            for q in range(1, RING):
                acc = acc + dot(oh[:, q * LANES : q * LANES + TOK], G[f][g][q * TOK : (q + 1) * TOK, cols])
            PK[f][g][:, cols] = acc.astype(BF16)
            return carry

        lax.fori_loop(0, width // 512, cols_step, 0)
        fold_out(PK[f][g], MAIN, es.at[f, g])

    def combine(f, g):
        lane = lax.broadcasted_iota(jnp.int32, (TOK, ROWS), 1)
        in_main = lane < MAIN
        block = jnp.where(in_main, lane // TOK, (lane - MAIN) // EXTRA)
        place = jnp.where(in_main, lax.rem(lane, TOK), TOK + lax.rem(lane - MAIN, EXTRA)).astype(F32)
        metas = (mo, mp)[g]
        for q in range(RING):
            m = jnp.concatenate([metas[f, q].astype(F32), jnp.zeros((LANES - 16, LANES), F32)], axis=0)
            m = m.T[0:TOK, :]
            s = m[:, 0:1]
            w = m[:, 4:5]
            for t in range(1, RING):
                s = jnp.where(block == t, m[:, t : t + 1], s)
                w = jnp.where(block == t, m[:, 4 + t : 5 + t], w)
            hit = jnp.logical_and(s >= 0, s + q * CAP == place)
            oh[q * TOK : (q + 1) * TOK, 0:ROWS] = jnp.where(hit, w, 0.0).astype(BF16)
        fold_in(yr.at[f, g], G[f][g], MAIN)

        def cols_step(j, carry):
            cols = aligned(j, 512)
            PK[f][g][0:MAIN, cols] = dot(oh[0:MAIN, 0:ROWS], G[f][g][:, cols]).astype(BF16)
            return carry

        lax.fori_loop(0, width // 512, cols_step, 0)

    def scatter_begin(f, g):
        axis, ref = AG_AXIS[g], PK[f][g]
        far = lax.rem(me[axis] + 2, RING)
        return [remote(slot_of(ref, far, LO), ra.at[f, g], peer(axis, 1)),
                remote(slot_of(ref, far, HI), rb.at[f, g], peer(axis, 3))]

    def scatter_relay(f, g, first):
        axis, ref = AG_AXIS[g], PK[f][g]
        m = me[axis]
        cps = []
        for i, (k, got, cols, dst) in enumerate(((1, ra, LO, rc), (3, rb, HI, rd))):
            first[i].wait_recv()
            c = lax.rem(m + k, RING)
            rows = pl.ds(pl.multiple_of(c * TOK, 16), TOK)
            ref[rows, cols] = (ref[rows, cols].astype(F32) + got[f, g].astype(F32)).astype(BF16)
            cps.append(remote(slot_of(ref, c), dst.at[f, g], peer(axis, k)))
        return cps

    def scatter_end(f, g, cps, more=None):
        axis, ref = AG_AXIS[g], PK[f][g]
        wait_recv(cps)
        rows = pl.ds(pl.multiple_of(me[axis] * TOK, 16), TOK)

        def cols_step(j, carry):
            cols = aligned(j, 512)
            acc = ref[rows, cols].astype(F32) + rc[f, g, :, cols].astype(F32) + rd[f, g, :, cols].astype(F32)
            if more is not None:
                acc = acc + more[:, cols].astype(F32)
            ref[rows, cols] = acc.astype(BF16)
            return carry

        lax.fori_loop(0, width // 512, cols_step, 0)

    own = [here(tok_hbm, slot_of(g_fo, y)), here(grd_hbm, slot_of(g_bo, y))]
    saved_in = [here(sg_hbm, hb.at[0 : TOK * 8, 0:inner]), here(su_hbm, hb.at[0 : TOK * 8, inner : 2 * inner])]
    begin(wa_pair)
    begin(wd_rows)

    barrier = pltpu.get_barrier_semaphore()
    everyone = [partner, next_sec, prev_sec] + [peer(a, k) for a in ("y", "x") for k in (1, 2, 3)]
    for device in everyone:
        pl.semaphore_signal(barrier, inc=1, device_id=device, device_id_type=MESH)
    pl.semaphore_wait(barrier, len(everyone))

    def tokens_begin(f):
        own[f].wait()
        to_z = remote(slot_of(G[f][O], y), slot_of(G[f][Q], x), partner)
        first = gather_begin("y", G[f][O])
        notes = [remote(meta.at[f, Q], mz.at[f], partner)]
        for k in (1, 2, 3):
            c = lax.rem(y + k, RING)
            notes.append(remote(meta.at[f, O, c], mo.at[f, y], at("y", c)))
        mo[f, y] = meta[f, O, y]
        return to_z, first, notes

    def partner_begin(f, to_z, notes):
        to_z.wait_recv()
        first = gather_begin("x", G[f][Q])
        notes[0].wait_recv()
        more = []
        for k in (1, 2, 3):
            c = lax.rem(x + k, RING)
            more.append(remote(mz.at[f, c], mp.at[f, x], at("x", c)))
        mp[f, x] = mz[f, x]
        return first, more

    def packed(f, g, sent, relays, notes):
        wait_recv(relays)
        wait_recv(notes)
        wait_send(sent + relays)
        pack(f, g)
        return exchange(UNI_AXIS[g], PK[f][g], 0, es.at[f, g], X[f], g * ROWS, er.at[f, g])

    z_f, o_f, n_f = tokens_begin(F)

    for cp in saved_in:
        cp.wait()
    for g, (dst, extra) in enumerate(((spk_o, spe.at[0]), (spk_p, spe.at[1]))):
        index = lax.broadcasted_iota(jnp.int32, (ROWS, TOK * 8), 0) + g * ROWS
        oh[...] = jnp.where(spos[...] == index, 1.0, 0.0).astype(BF16)

        def cols_step(j, carry):
            cols = aligned(j, 512)
            dst[:, cols] = dot(oh[...], hb[0 : TOK * 8, cols]).astype(BF16)
            return carry

        lax.fori_loop(0, 2 * inner // 512, cols_step, 0)
        fold_out(dst, MAIN, extra)

    ro_f = gather_relay("y", g_fo, o_f)
    p_f, np_f = partner_begin(F, z_f, n_f)
    z_b, o_b, n_b = tokens_begin(B)
    uo_f, lo_f = packed(F, O, [z_f] + o_f, ro_f, n_f[1:])
    s1_o, sl_o = exchange("y", spk_o, 0, spe.at[0], sg_o, 0, sge.at[0])
    s1_z = [remote(spk_p.at[0:MAIN, :], sz, partner), remote(spe.at[1], sze, partner)]
    rp_f = gather_relay("x", g_fp, p_f)
    ro_b = gather_relay("y", g_bo, o_b)
    up_f, lp_f = packed(F, Q, p_f, rp_f, np_f)
    p_b, np_b = partner_begin(B, z_b, n_b)
    wait_recv(s1_z)
    s1_p, sl_p = exchange("x", sz, 0, sze, sg_p, 0, sge.at[1])
    uo_b, lo_b = packed(B, O, [z_b] + o_b, ro_b, n_b[1:])
    rp_b = gather_relay("x", g_bp, p_b)

    def saved_second(g, first, own_copy, before, got, out):
        wait_recv(first)
        own_copy.wait()
        wait_send(before)
        fold_in(sge.at[g], got, MAIN)

        def cols_step(j, carry):
            cols = aligned(j, 512)
            out[:, cols] = dot(swap[...], got[:, cols]).astype(BF16)
            return carry

        lax.fori_loop(0, 2 * inner // 512, cols_step, 0)
        fold_out(out, MAIN, s2e.at[g])
        return exchange(UNI_AXIS[g], out, 0, s2e.at[g], sx, g * ROWS, sxe.at[g])

    s2_o, sm_o = saved_second(O, s1_o, sl_o, s1_o, sg_o, spk_o)
    up_b, lp_b = packed(B, Q, p_b, rp_b, np_b)
    s2_p, sm_p = saved_second(Q, s1_p, sl_p, s1_z, sg_p, spk_p)

    wait_recv(uo_f + up_f)
    lo_f.wait()
    lp_f.wait()
    for g in (O, Q):
        fold_in(er.at[F, g], x_f, g * ROWS + MAIN)

    def fwd_hidden(j, slot):
        for r in range(2):
            rows = slice(r * ROWS, (r + 1) * ROWS)
            both = dot(x_f[rows, :], wa[slot])
            gate, up = both[:, 0:LANES], both[:, LANES : 2 * LANES]
            hb[rows, aligned(j, LANES)] = (gate / (1.0 + jnp.exp(-gate)) * up).astype(BF16)

    stream(inner // LANES, wa_pair, fwd_hidden)
    begin(wa_down)

    def fwd_down(j, slot):
        for r in range(2):
            rows = slice(r * ROWS, (r + 1) * ROWS)
            x_f[rows, aligned(j, 256)] = dot(hb[rows, 0:inner], wa[slot, 0:inner, :]).astype(BF16)

    stream(width // 256, wa_down, fwd_down)

    def give_back(f):
        cps, owns = [], []
        for g in (O, Q):
            fold_out(X[f], g * ROWS + MAIN, ys.at[f, g])
            c, o = exchange(UNI_AXIS[g], X[f], g * ROWS, ys.at[f, g], G[f][g], 0, yr.at[f, g])
            cps.append(c)
            owns.append(o)
        return cps, owns

    back_f, own_f = give_back(F)

    wait_recv(uo_b + up_b + s2_o + s2_p)
    for cp in (lo_b, lp_b, sm_o, sm_p):
        cp.wait()
    for g in (O, Q):
        fold_in(er.at[B, g], x_b, g * ROWS + MAIN)
        fold_in(sxe.at[g], sx, g * ROWS + MAIN)

    def bwd_hidden(j, slot):
        cols, more = aligned(j, 256), pl.ds(pl.multiple_of(inner + j * 256, 256), 256)
        for r in range(2):
            rows = slice(r * ROWS, (r + 1) * ROWS)
            grad = dot_t(x_b[rows, :], wd_t[slot])
            a = sx[rows, cols].astype(F32)
            b = sx[rows, more].astype(F32)
            s = 1.0 / (1.0 + jnp.exp(-a))
            hb[rows, cols] = (grad * b * s * (1.0 + a * (1.0 - s))).astype(BF16)
            hb[rows, more] = (grad * a * s).astype(BF16)

    stream(inner // 256, wd_rows, bwd_hidden)
    begin(wd_pair)

    def bwd_down(j, slot):
        for r in range(2):
            rows = slice(r * ROWS, (r + 1) * ROWS)
            x_b[rows, aligned(j, 256)] = dot_t(hb[rows, :], wd_t[slot, :, 0 : 2 * inner]).astype(BF16)

    stream(width // 256, wd_pair, bwd_down)

    back_b, own_b = give_back(B)

    def sums_begin(f, g, back, own_copy, before):
        wait_recv(back)
        own_copy.wait()
        wait_send(before)
        combine(f, g)
        return scatter_begin(f, g)

    def sums(f, back, owns, before, out, device):
        first_p = sums_begin(f, Q, back[Q], owns[Q], before[Q])
        first_o = sums_begin(f, O, back[O], owns[O], before[O])
        second_p = scatter_relay(f, Q, first_p)
        second_o = scatter_relay(f, O, first_o)
        scatter_end(f, Q, second_p)
        home = remote(slot_of(PK[f][Q], x), zr.at[f], partner)
        home.wait_recv()
        scatter_end(f, O, second_o, zr.at[f])
        last = remote(slot_of(PK[f][O], y), out, device)
        return first_p + first_o + second_p + second_o + [home], last

    sent_f, last_f = sums(F, back_f, own_f, (uo_f, up_f), out_f, next_sec)
    sent_b, last_b = sums(B, back_b, own_b, (uo_b, up_b), out_b, prev_sec)

    wait_send(sent_f + sent_b + back_f[0] + back_f[1] + back_b[0] + back_b[1])
    wait_send(n_f + np_f + n_b + np_b + s1_p + s2_o + s2_p)
    last_f.wait()
    last_b.wait()


def place_notes(routes, gates, e):
    expert = jnp.arange(32, dtype=jnp.int32)
    hot = routes.T[None, :, :] == expert[:, None, None]
    named = jnp.any(hot, axis=1)
    count = named.astype(F32)
    earlier = jnp.asarray(np.triu(np.ones((TOK, TOK), np.float32), 1))
    within = jnp.dot(count, earlier, preferred_element_type=F32)
    slot = jnp.where(named, within, -1.0)
    gate = jnp.sum(jnp.where(hot, gates.T[None, :, :], 0.0), axis=1)
    z = e // 16
    out = []
    slots = slot.reshape(2, 4, 4, TOK)
    gates_ = gate.reshape(2, 4, 4, TOK)
    for plane, flip in ((z, False), (1 - z, True)):
        s = lax.dynamic_index_in_dim(slots, plane, 0, keepdims=False)
        w = lax.dynamic_index_in_dim(gates_, plane, 0, keepdims=False)
        if flip:
            s, w = s.transpose(1, 0, 2), w.transpose(1, 0, 2)
        both = jnp.concatenate([s, w, jnp.full((4, 8, TOK), -1.0, F32)], axis=1)
        out.append(jnp.pad(both, ((0, 0), (0, 0), (0, LANES - TOK)), constant_values=-1.0))
    return jnp.stack(out).astype(BF16), hot, within


def saved_places(routes, hot, within, e):
    slot = jnp.sum(jnp.where(hot, within[:, None, :], 0.0), axis=0).T.astype(jnp.int32)
    z = e // 16
    there, ey, ex = routes // 16, lax.rem(routes // 4, 4), lax.rem(routes, 4)
    same = there == z
    block = jnp.where(same, ey, ex)
    place = jnp.where(same, ex, ey) * CAP + slot
    row = jnp.where(place < TOK, block * TOK + place, MAIN + block * EXTRA + place - TOK)
    return (row + jnp.where(same, 0, ROWS)).reshape(1, -1)


def body(
    fwd_tokens,
    fwd_routes,
    fwd_gates,
    bwd_grads,
    bwd_routes,
    bwd_gates,
    saved_gate,
    saved_up,
    w_gate,
    w_up,
    w_down,
):
    e = lax.axis_index("expert")
    tokens, grads = fwd_tokens[0], bwd_grads[0]
    width, inner = tokens.shape[1], w_gate.shape[3]
    note_f, _, _ = place_notes(fwd_routes[0], fwd_gates[0], e)
    note_b, hot, within = place_notes(bwd_routes[0], bwd_gates[0], e)
    meta = jnp.stack([note_f, note_b])
    spos = saved_places(bwd_routes[0], hot, within, e)
    quarter = width // 4
    any_, vmem = pl.BlockSpec(memory_space=pl.ANY), pl.BlockSpec(memory_space=pltpu.VMEM)

    def buf(*shape):
        return pltpu.VMEM(shape, BF16)

    scratch = (
        [buf(ROWS, width)] * 8
        + [buf(2 * ROWS, width)] * 2
        + [buf(2, 2, 4 * TAIL, quarter)] * 4
        + [buf(2, 2, TOK, width // 2)] * 2
        + [buf(2, 2, TOK, width)] * 2
        + [buf(2, TOK, width)]
        + [buf(2, 4, 16, LANES)] * 3
        + [buf(ROWS, 2 * inner)] * 4
        + [buf(MAIN, 2 * inner), buf(2 * ROWS, 2 * inner)]
        + [buf(2, 4 * TAIL, inner // 2)] * 2
        + [buf(4 * TAIL, inner // 2)]
        + [buf(2, 4 * TAIL, inner // 2)] * 2
        + [buf(2 * ROWS, 2 * inner), buf(ROWS, TOK * 8)]
        + [buf(2, width, 256), buf(2, 256, width)]
        + [pltpu.SemaphoreType.DMA((N_SEMS,)), pltpu.SemaphoreType.DMA((N_SEMS,))]
        + [pltpu.SemaphoreType.DMA((N_LOCAL,)), pltpu.SemaphoreType.DMA((4, 2))]
    )
    out = jax.ShapeDtypeStruct(tokens.shape, BF16)
    rows = 2 * ROWS
    next_inputs, prev_grads = pl.pallas_call(
        kernel,
        out_shape=(out, out),
        in_specs=[any_] * 7 + [vmem] * 4,
        out_specs=(any_, any_),
        scratch_shapes=scratch,
        compiler_params=pltpu.CompilerParams(
            collective_id=1, has_side_effects=True, vmem_limit_bytes=62 * 1024 * 1024
        ),
        cost_estimate=pl.CostEstimate(
            flops=12 * rows * width * inner, bytes_accessed=12 * width * inner, transcendentals=2 * rows * inner
        ),
    )(
        tokens,
        grads,
        saved_gate[0].reshape(-1, inner),
        saved_up[0].reshape(-1, inner),
        w_gate[0, 0],
        w_up[0, 0],
        w_down[0, 0],
        meta,
        spos,
        jnp.asarray(fold_matrix(), BF16),
        jnp.asarray(swap_matrix(), BF16),
    )
    return (next_inputs[None], prev_grads[None])


def solution(mesh):
    return jax.shard_map(
        body,
        mesh=mesh,
        in_specs=(P("section", "expert", None),) * 6 + (P("section", "expert", None, None),) * 5,
        out_specs=(P("section", "expert", None), P("section", "expert", None)),
        check_vma=False,
    )
```

```python
import functools

import jax
import jax.numpy as jnp
import numpy as np
from jax import lax
from jax.experimental import pallas as pl
from jax.experimental.pallas import tpu as pltpu
from jax.sharding import PartitionSpec as P

MESH = pl.DeviceIdType.MESH
F32 = jnp.float32
BF16 = jnp.bfloat16

RING = 4
CAP = 21
TOK = 80
GROUP = RING * CAP
EXTRA = GROUP - TOK
MAIN = RING * TOK
ROWS = RING * GROUP
TAIL = ROWS - MAIN
LANES = 128
N_SEMS = 176
N_LOCAL = 24


def row_of(block, place):
    return block * TOK + place if place < TOK else MAIN + block * EXTRA + place - TOK


def swap_matrix():
    m = np.zeros((ROWS, ROWS), np.float32)
    for q in range(RING):
        for t in range(RING):
            for i in range(CAP):
                m[row_of(t, q * CAP + i), row_of(q, t * CAP + i)] = 1
    return m


def fold_matrix():
    m = np.zeros((4 * TAIL, 4 * TAIL), np.float32)
    for a in range(4):
        for b in range(4):
            for j in range(4):
                m[b * 16 + a * 4 + j, a * 16 + b * 4 + j] = 1
    return m


def dot(a, b):
    return jnp.dot(a, b, preferred_element_type=F32)


def dot_t(a, b):
    return lax.dot_general(a, b, (((1,), (1,)), ((), ())), preferred_element_type=F32)


def aligned(i, size):
    return pl.ds(pl.multiple_of(i * size, size), size)


def kernel(
    tok_hbm,
    grd_hbm,
    sg_hbm,
    su_hbm,
    wg_hbm,
    wu_hbm,
    wd_hbm,
    routes_f, gates_f, routes_b, gates_b,
    fold,
    swap,
    out_fo, out_fp, out_bo, out_bp,
    g_fo, g_fp, g_bo, g_bp,
    pk_fo, pk_fp, pk_bo, pk_bp,
    x_f, x_b,
    es, er, ys, yr,
    ra, rb, rc, rd, zr,
    meta, mo, mz, mp, turn, spos,
    spk_o, spk_p, sg_o, sg_p, sz, sx,
    spe, sge, sze, s2e, sxe,
    hb, oh, qm, gc, wa, wd_t,
    send, recv, local, wsem,
):
    e = lax.axis_index("expert")
    sec = lax.axis_index("section")
    n_sec = lax.axis_size("section")
    z, y, x = e // 16, lax.rem(e // 4, 4), lax.rem(e, 4)
    me = {"y": y, "x": x}
    width = tok_hbm.shape[1]
    inner = wg_hbm.shape[1]
    half = width // 2
    F, B, O, Q = 0, 1, 0, 1
    G = ((g_fo, g_fp), (g_bo, g_bp))
    PK = ((pk_fo, pk_fp), (pk_bo, pk_bp))
    X = (x_f, x_b)
    AG_AXIS = (("y", "x"), ("x", "y"))
    UNI_AXIS = (("x", "y"), ("y", "x"))
    CHUNKS = ((0, 2048), (2048, width - 2048))

    def at(axis, c):
        if axis == "y":
            return (sec, z * 16 + c * 4 + x)
        return (sec, z * 16 + y * 4 + c)

    def peer(axis, k):
        return at(axis, lax.rem(me[axis] + k, RING))

    other = (1 - z) * 16 + y * 4 + x
    partner = (sec, other)
    next_sec = lax.rem(sec + 1, n_sec)
    prev_sec = lax.rem(sec + n_sec - 1, n_sec)

    used = [0, 0]

    def remote(src, dst, device):
        i = used[0]
        used[0] += 1
        cp = pltpu.make_async_remote_copy(
            src_ref=src, dst_ref=dst, send_sem=send.at[i], recv_sem=recv.at[i],
            device_id=device, device_id_type=MESH,
        )
        cp.start()
        return cp

    def here(src, dst):
        i = used[1]
        used[1] += 1
        cp = pltpu.make_async_copy(src, dst, local.at[i])
        cp.start()
        return cp

    def wait_recv(cps):
        for cp in cps:
            cp.wait_recv()

    def wait_send(cps):
        for cp in cps:
            cp.wait_send()

    def turned(ref, fill):
        turn[...] = jnp.full((8, LANES), fill, F32)
        turn[:, 0:TOK] = ref[...].astype(F32)
        return turn[...]

    def places(f, routes, gates):
        named_by = turned(routes, -1.0)
        gate_by = turned(gates, 0.0)
        expert = lax.broadcasted_iota(jnp.int32, (32, LANES), 0).astype(F32)
        hot = [named_by[k : k + 1, :] == expert for k in range(8)]
        count = jnp.zeros((32, LANES), F32)
        gate = jnp.zeros((32, LANES), F32)
        for k in range(8):
            count += jnp.where(hot[k], 1.0, 0.0)
            gate += jnp.where(hot[k], gate_by[k : k + 1, :], 0.0)
        earlier = lax.broadcasted_iota(jnp.int32, (LANES, LANES), 0) < lax.broadcasted_iota(jnp.int32, (LANES, LANES), 1)
        within = dot(count.astype(BF16), jnp.where(earlier, 1.0, 0.0).astype(BF16))
        high = gate.astype(BF16).astype(F32)
        rows = jnp.concatenate([jnp.where(count > 0, within, -1.0), high, gate - high], axis=0).astype(BF16)
        r = lax.broadcasted_iota(jnp.int32, (64, 96), 0)
        message, kind, item = r // 16, lax.rem(r, 16) // 4, lax.rem(r, 4)
        col = lax.broadcasted_iota(jnp.int32, (64, 96), 1)
        for g in (O, Q):
            plane = z if g == O else 1 - z
            if AG_AXIS[f][g] == "y":
                index = plane * 16 + message * 4 + item
            else:
                index = plane * 16 + item * 4 + message
            pick = jnp.where(jnp.logical_and(kind < 3, col == kind * 32 + index), 1.0, 0.0).astype(BF16)
            got = dot(pick, rows).astype(BF16)
            for c in range(4):
                meta[f, g, c] = got[c * 16 : (c + 1) * 16, :]
        if f == F:
            return
        slot = jnp.concatenate(
            [jnp.sum(jnp.where(hot[k], within, 0.0), axis=0, keepdims=True) for k in range(8)], axis=0
        ).astype(jnp.int32)
        chosen = named_by.astype(jnp.int32)
        same = chosen // 16 == z
        cy, cx = lax.rem(chosen // 4, 4), lax.rem(chosen, 4)
        block = jnp.where(same, cx, cy)
        place = jnp.where(same, cy, cx) * CAP + slot
        row = jnp.where(place < TOK, block * TOK + place, MAIN + block * EXTRA + place - TOK)
        row = row + jnp.where(same, 0, ROWS)
        token = lax.broadcasted_iota(jnp.int32, (LANES, TOK * 8), 0)
        lane = lax.broadcasted_iota(jnp.int32, (LANES, TOK * 8), 1)
        spread = jnp.where(lane // 8 == token, 1.0, 0.0).astype(BF16)
        coarse = (row // 16).astype(F32).astype(BF16)
        fine = lax.rem(row, 16).astype(F32).astype(BF16)
        wide = 16.0 * dot(coarse, spread) + dot(fine, spread)
        mine = lax.broadcasted_iota(jnp.int32, (8, TOK * 8), 0) == lax.rem(lane[0:8, :], 8)
        total = jnp.sum(jnp.where(mine, wide, 0.0), axis=0, keepdims=True)
        spos[...] = jnp.broadcast_to(total, (8, TOK * 8))

    def wa_pair(j, slot):
        cols = pl.ds(pl.multiple_of(j * LANES, LANES), LANES)
        return (
            pltpu.make_async_copy(wg_hbm.at[:, cols], wa.at[slot, :, 0:LANES], wsem.at[0, slot]),
            pltpu.make_async_copy(wu_hbm.at[:, cols], wa.at[slot, :, LANES : 2 * LANES], wsem.at[1, slot]),
        )

    def wa_down(j, slot):
        cols = pl.ds(pl.multiple_of(j * 256, 256), 256)
        return (pltpu.make_async_copy(wd_hbm.at[:, cols], wa.at[slot, 0:inner, :], wsem.at[0, slot]),)

    def wd_rows(j, slot):
        rows = aligned(j, 256)
        return (pltpu.make_async_copy(wd_hbm.at[rows, :], wd_t.at[slot], wsem.at[2, slot]),)

    def wd_pair(j, slot):
        rows = aligned(j, 256)
        return (
            pltpu.make_async_copy(wg_hbm.at[rows, :], wd_t.at[slot, :, 0:inner], wsem.at[2, slot]),
            pltpu.make_async_copy(wu_hbm.at[rows, :], wd_t.at[slot, :, inner : 2 * inner], wsem.at[3, slot]),
        )

    def begin(tiles):
        for cp in tiles(0, 0):
            cp.start()

    def stream(n, tiles, work, first=0, last=None):
        def step(j, carry):
            slot = lax.rem(j, 2)

            @pl.when(j + 1 < n)
            def _():
                for cp in tiles(j + 1, 1 - slot):
                    cp.start()

            for cp in tiles(j, slot):
                cp.wait()
            work(j, slot)
            return carry

        lax.fori_loop(first, n if last is None else last, step, 0)

    def fold_out(src, row0, dst, col0=0, size=None):
        w4 = (src.shape[1] if size is None else size) // 4
        a = jnp.concatenate(
            [src[row0 : row0 + TAIL, col0 + c * w4 : col0 + (c + 1) * w4] for c in range(4)], axis=0)
        dst[...] = dot(fold[...], a).astype(BF16)

    def fold_in(src, dst, row0, col0=0, size=None):
        w4 = (dst.shape[1] if size is None else size) // 4
        a = dot(fold[...], src[...]).astype(BF16)
        for c in range(4):
            dst[row0 : row0 + TAIL, col0 + c * w4 : col0 + (c + 1) * w4] = a[c * TAIL : (c + 1) * TAIL, :]

    def exchange(axis, src, src_off, src_extra, dst, dst_off, dst_extra, cols=slice(None)):
        m = me[axis]
        cps = []
        for k in (2, 1, 3):
            c = lax.rem(m + k, RING)
            cps.append(remote(
                src.at[pl.ds(pl.multiple_of(src_off + c * TOK, 16), TOK), cols],
                dst.at[pl.ds(pl.multiple_of(dst_off + m * TOK, 16), TOK), cols],
                at(axis, c)))
            cps.append(remote(src_extra.at[aligned(c, TAIL), :], dst_extra.at[aligned(m, TAIL), :], at(axis, c)))
        own = here(
            src.at[pl.ds(pl.multiple_of(src_off + m * TOK, 16), TOK), cols],
            dst.at[pl.ds(pl.multiple_of(dst_off + m * TOK, 16), TOK), cols])
        dst_extra[aligned(m, TAIL), :] = src_extra[aligned(m, TAIL), :]
        return cps, own

    def slot_of(ref, c, cols=None):
        rows = pl.ds(pl.multiple_of(c * TOK, 16), TOK)
        return ref.at[rows, :] if cols is None else ref.at[rows, cols]

    LO, HI = pl.ds(0, half), pl.ds(half, half)

    def gather_begin(axis, ref):
        m = me[axis]
        return [remote(slot_of(ref, m), slot_of(ref, m), peer(axis, 1)),
                remote(slot_of(ref, m), slot_of(ref, m), peer(axis, 3))]

    def gather_relay(axis, ref, first):
        m = me[axis]
        before, after = lax.rem(m + 3, RING), lax.rem(m + 1, RING)
        first[0].wait_recv()
        a = remote(slot_of(ref, before, LO), slot_of(ref, before, LO), peer(axis, 1))
        first[1].wait_recv()
        b = remote(slot_of(ref, after, HI), slot_of(ref, after, HI), peer(axis, 3))
        return [a, b]

    def pack(f, g):
        wide = lax.broadcasted_iota(jnp.int32, (TOK, LANES), 0).astype(F32)
        tail = lax.broadcasted_iota(jnp.int32, (TAIL, LANES), 0)
        tail_place = (TOK + lax.rem(tail, EXTRA)).astype(F32)
        tail_block = tail // EXTRA
        metas = (mo, mp)[g]
        gate = [jnp.zeros((TOK, 1), F32)] * RING
        tail_gate = jnp.zeros((TAIL, 1), F32)
        for q in range(RING):
            m = metas[f, q].astype(F32)
            s = jnp.where(m >= 0, m + q * CAP, -1.0)
            w = m[4:8, :] + m[8:12, :]
            cols = slice(q * LANES, (q + 1) * LANES)
            chosen = jnp.zeros((TAIL, LANES), F32)
            weight = jnp.zeros((TAIL, LANES), F32)
            for t in range(RING):
                row, w_row = s[t : t + 1, :], w[t : t + 1, :]
                hit = wide == row
                oh[t * TOK : (t + 1) * TOK, cols] = jnp.where(hit, 1.0, 0.0).astype(BF16)
                chosen = jnp.where(tail_block == t, row, chosen)
                if f == B:
                    gate[t] += jnp.sum(jnp.where(hit, w_row, 0.0), axis=1, keepdims=True)
                    weight = jnp.where(tail_block == t, w_row, weight)
            hit = chosen == tail_place
            oh[MAIN:ROWS, cols] = jnp.where(hit, 1.0, 0.0).astype(BF16)
            tail_gate += jnp.sum(jnp.where(hit, weight, 0.0), axis=1, keepdims=True)
        if f == B:
            for t in range(RING):
                gc[t * TOK : (t + 1) * TOK, :] = jnp.broadcast_to(gate[t], (TOK, LANES))
            gc[MAIN:ROWS, :] = jnp.broadcast_to(tail_gate, (TAIL, LANES))

        def cols_step(j, carry):
            cols = aligned(j, 512)
            acc = dot(oh[:, 0:TOK], G[f][g][0:TOK, cols])
            for q in range(1, RING):
                acc = acc + dot(oh[:, q * LANES : q * LANES + TOK], G[f][g][q * TOK : (q + 1) * TOK, cols])
            if f == B:
                acc = acc * gc[:, 0:1]
            PK[f][g][:, cols] = acc.astype(BF16)
            return carry

        lax.fori_loop(0, width // 512, cols_step, 0)
        fold_out(PK[f][g], MAIN, es.at[f, g])

    def weights(f, g):
        lane = lax.broadcasted_iota(jnp.int32, (TOK, ROWS), 1)
        in_main = lane < MAIN
        block = jnp.where(in_main, lane // TOK, (lane - MAIN) // EXTRA)
        place = jnp.where(in_main, lax.rem(lane, TOK), TOK + lax.rem(lane - MAIN, EXTRA)).astype(F32)
        metas = (mo, mp)[g]
        for q in range(RING):
            m = jnp.concatenate([metas[f, q].astype(F32), jnp.zeros((LANES - 16, LANES), F32)], axis=0)
            m = m.T[0:TOK, :]
            s = m[:, 0:1]
            w = m[:, 4:5]
            for t in range(1, RING):
                s = jnp.where(block == t, m[:, t : t + 1], s)
                w = jnp.where(block == t, m[:, 4 + t : 5 + t], w)
            hit = jnp.logical_and(s >= 0, s + q * CAP == place)
            qm[f, g, q * TOK : (q + 1) * TOK, :] = jnp.where(hit, w if f == F else 1.0, 0.0).astype(BF16)

    def combine(f, g, h):
        col0, size = CHUNKS[h]
        fold_in(yr.at[f, g, :, pl.ds(col0 // 4, size // 4)], G[f][g], MAIN, col0, size)

        def cols_step(j, carry):
            cols = aligned(j, 512)
            PK[f][g][0:MAIN, cols] = dot(qm[f, g], G[f][g][:, cols]).astype(BF16)
            return carry

        lax.fori_loop(col0 // 512, (col0 + size) // 512, cols_step, 0)

    def parts(h):
        col0, size = CHUNKS[h]
        return (pl.ds(col0, size // 2), pl.ds(col0 + size // 2, size // 2)), pl.ds(col0 // 2, size // 2), pl.ds(col0, size)

    def scatter_begin(f, g, h):
        axis, ref = AG_AXIS[f][g], PK[f][g]
        (lo, hi), short, _ = parts(h)
        far = lax.rem(me[axis] + 2, RING)
        return [remote(slot_of(ref, far, lo), ra.at[f, g, :, short], peer(axis, 1)),
                remote(slot_of(ref, far, hi), rb.at[f, g, :, short], peer(axis, 3))]

    def scatter_relay(f, g, h, first):
        axis, ref = AG_AXIS[f][g], PK[f][g]
        ends, short, whole = parts(h)
        m = me[axis]
        cps = []
        for i, (k, got, dst) in enumerate(((1, ra, rc), (3, rb, rd))):
            first[i].wait_recv()
            c = lax.rem(m + k, RING)
            rows = pl.ds(pl.multiple_of(c * TOK, 16), TOK)
            ref[rows, ends[i]] = (ref[rows, ends[i]].astype(F32) + got[f, g, :, short].astype(F32)).astype(BF16)
            cps.append(remote(slot_of(ref, c, whole), dst.at[f, g, :, whole], peer(axis, k)))
        return cps

    def scatter_end(f, g, h, cps, out, device):
        axis, ref = AG_AXIS[f][g], PK[f][g]
        col0, size = CHUNKS[h]
        wait_recv(cps)
        rows = pl.ds(pl.multiple_of(me[axis] * TOK, 16), TOK)

        def cols_step(j, carry):
            cols = aligned(j, 512)
            acc = ref[rows, cols].astype(F32) + rc[f, g, :, cols].astype(F32) + rd[f, g, :, cols].astype(F32)
            ref[rows, cols] = acc.astype(BF16)
            return carry

        lax.fori_loop(col0 // 512, (col0 + size) // 512, cols_step, 0)
        whole = pl.ds(col0, size)
        return remote(slot_of(ref, me[axis], whole), out.at[:, whole], device)

    own = [here(tok_hbm, slot_of(g_fo, y)), here(grd_hbm, slot_of(g_bo, x))]
    saved_in = [here(sg_hbm, hb.at[0 : TOK * 8, 0:inner]), here(su_hbm, hb.at[0 : TOK * 8, inner : 2 * inner])]
    begin(wa_pair)
    begin(wd_rows)

    barrier = pltpu.get_barrier_semaphore()
    everyone = [partner, (next_sec, e), (prev_sec, e), (next_sec, other), (prev_sec, other)]
    everyone += [peer(a, k) for a in ("y", "x") for k in (1, 2, 3)]
    for device in everyone:
        pl.semaphore_signal(barrier, inc=1, device_id=device, device_id_type=MESH)
    pl.semaphore_wait(barrier, len(everyone))

    def gather_first(f):
        own[f].wait()
        return gather_begin(AG_AXIS[f][O], G[f][O])

    def partner_send(f):
        return remote(slot_of(G[f][O], me[AG_AXIS[f][O]]), slot_of(G[f][Q], me[AG_AXIS[f][Q]]), partner)

    def notes_begin(f):
        axis = AG_AXIS[f][O]
        m = me[axis]
        notes = [remote(meta.at[f, Q], mz.at[f], partner)]
        for k in (1, 2, 3):
            c = lax.rem(m + k, RING)
            notes.append(remote(meta.at[f, O, c], mo.at[f, m], at(axis, c)))
        mo[f, m] = meta[f, O, m]
        return notes

    def partner_begin(f, to_z, notes):
        axis = AG_AXIS[f][Q]
        m = me[axis]
        to_z.wait_recv()
        first = gather_begin(axis, G[f][Q])
        notes[0].wait_recv()
        more = []
        for k in (1, 2, 3):
            c = lax.rem(m + k, RING)
            more.append(remote(mz.at[f, c], mp.at[f, m], at(axis, c)))
        mp[f, m] = mz[f, m]
        return first, more

    def packed(f, g, sent, relays, notes):
        wait_recv(notes)
        wait_recv(relays)
        wait_send(sent + relays)
        pack(f, g)
        return exchange(UNI_AXIS[f][g], PK[f][g], 0, es.at[f, g], X[f], g * ROWS, er.at[f, g])

    def saved_pack(g, dst):
        index = (lax.broadcasted_iota(jnp.int32, (ROWS, TOK * 8), 0) + g * ROWS).astype(F32)
        oh[...] = jnp.where(spos[0:1, :] == index, 1.0, 0.0).astype(BF16)

        def cols_step(j, carry):
            cols = aligned(j, 512)
            dst[:, cols] = dot(oh[...], hb[0 : TOK * 8, cols]).astype(BF16)
            return carry

        lax.fori_loop(0, 2 * inner // 512, cols_step, 0)
        fold_out(dst, MAIN, spe.at[g])

    o_f = gather_first(F)
    z_f = partner_send(F)
    o_b = gather_first(B)
    places(F, routes_f, gates_f)
    n_f = notes_begin(F)
    places(B, routes_b, gates_b)
    n_b = notes_begin(B)
    for cp in saved_in:
        cp.wait()
    saved_pack(Q, spk_p)
    ro_f = gather_relay("y", g_fo, o_f)
    ro_b = gather_relay("x", g_bo, o_b)
    p_f, np_f = partner_begin(F, z_f, n_f)
    z_b = partner_send(B)
    uo_f, lo_f = packed(F, O, [z_f] + o_f, ro_f, n_f[1:])
    uo_b, lo_b = packed(B, O, [z_b] + o_b, ro_b, n_b[1:])
    p_b, np_b = partner_begin(B, z_b, n_b)
    s1_z = [remote(spk_p.at[0:MAIN, :], sz, partner), remote(spe.at[1], sze, partner)]
    rp_f = gather_relay("x", g_fp, p_f)
    saved_pack(O, spk_o)
    s1_o, sl_o = exchange("x", spk_o, 0, spe.at[0], sg_o, 0, sge.at[0])
    weights(F, O)
    up_f, lp_f = packed(F, Q, p_f, rp_f, np_f)
    rp_b = gather_relay("y", g_bp, p_b)
    weights(F, Q)
    up_b, lp_b = packed(B, Q, p_b, rp_b, np_b)
    wait_recv(s1_z)
    s1_p, sl_p = exchange("y", sz, 0, sze, sg_p, 0, sge.at[1])

    def saved_second(g, first, own_copy, before, got, out):
        wait_recv(first)
        own_copy.wait()
        wait_send(before)
        fold_in(sge.at[g], got, MAIN)

        def cols_step(j, carry):
            cols = aligned(j, 512)
            out[:, cols] = dot(swap[...], got[:, cols]).astype(BF16)
            return carry

        lax.fori_loop(0, 2 * inner // 512, cols_step, 0)
        fold_out(out, MAIN, s2e.at[g])
        return exchange(UNI_AXIS[B][g], out, 0, s2e.at[g], sx, g * ROWS, sxe.at[g])

    s2_o, sm_o = saved_second(O, s1_o, sl_o, s1_o, sg_o, spk_o)
    weights(B, O)
    weights(B, Q)

    wait_recv(uo_f + up_f)
    lo_f.wait()
    lp_f.wait()
    for g in (O, Q):
        fold_in(er.at[F, g], x_f, g * ROWS + MAIN)

    def fwd_hidden(j, slot):
        for r in range(2):
            rows = slice(r * ROWS, (r + 1) * ROWS)
            both = dot(x_f[rows, :], wa[slot])
            gate, up = both[:, 0:LANES], both[:, LANES : 2 * LANES]
            hb[rows, aligned(j, LANES)] = (gate / (1.0 + jnp.exp(-gate)) * up).astype(BF16)

    stream(inner // LANES, wa_pair, fwd_hidden)
    begin(wa_down)
    s2_p, sm_p = saved_second(Q, s1_p, sl_p, s1_z, sg_p, spk_p)

    def fwd_down(j, slot):
        for r in range(2):
            rows = slice(r * ROWS, (r + 1) * ROWS)
            x_f[rows, aligned(j, 256)] = dot(hb[rows, 0:inner], wa[slot, 0:inner, :]).astype(BF16)

    def give_back(f, h):
        col0, size = CHUNKS[h]
        cps, owns = [], []
        for g in (Q, O):
            extra = (f, g, slice(None), pl.ds(col0 // 4, size // 4))
            fold_out(X[f], g * ROWS + MAIN, ys.at[extra], col0, size)
            c, o = exchange(
                UNI_AXIS[f][g], X[f], g * ROWS, ys.at[extra], G[f][g], 0, yr.at[extra], pl.ds(col0, size))
            cps = cps + c
            owns.append(o)
        return cps, owns

    tiles = width // 256
    cut = CHUNKS[0][1] // 256
    stream(tiles, wa_down, fwd_down, 0, cut)
    back_f0 = give_back(F, 0)
    stream(tiles, wa_down, fwd_down, cut, tiles)
    back_f1 = give_back(F, 1)

    wait_recv(uo_b + up_b + s2_o + s2_p)
    for cp in (lo_b, lp_b, sm_o, sm_p):
        cp.wait()
    for g in (O, Q):
        fold_in(er.at[B, g], x_b, g * ROWS + MAIN)
        fold_in(sxe.at[g], sx, g * ROWS + MAIN)

    def bwd_hidden(j, slot):
        cols, more = aligned(j, 256), pl.ds(pl.multiple_of(inner + j * 256, 256), 256)
        for r in range(2):
            rows = slice(r * ROWS, (r + 1) * ROWS)
            grad = dot_t(x_b[rows, :], wd_t[slot])
            a = sx[rows, cols].astype(F32)
            b = sx[rows, more].astype(F32)
            s = 1.0 / (1.0 + jnp.exp(-a))
            hb[rows, cols] = (grad * b * s * (1.0 + a * (1.0 - s))).astype(BF16)
            hb[rows, more] = (grad * a * s).astype(BF16)

    stream(inner // 256, wd_rows, bwd_hidden)
    begin(wd_pair)

    def bwd_down(j, slot):
        for r in range(2):
            rows = slice(r * ROWS, (r + 1) * ROWS)
            x_b[rows, aligned(j, 256)] = dot_t(hb[rows, :], wd_t[slot, :, 0 : 2 * inner]).astype(BF16)

    def sums_begin(f, h, back, before):
        cps, owns = back
        wait_recv(cps)
        for cp in owns:
            cp.wait()
        wait_send(before)
        first = {}
        for g in (Q, O):
            combine(f, g, h)
            first[g] = scatter_begin(f, g, h)
        return first

    def sums_relay(f, h, first):
        return {g: scatter_relay(f, g, h, first[g]) for g in (Q, O)}

    outs = ((out_fo, out_fp), (out_bo, out_bp))
    to_sec = (next_sec, prev_sec)

    def sums_end(f, h, second):
        return [scatter_end(f, g, h, second[g], outs[f][g], (to_sec[f], (e, other)[g])) for g in (Q, O)]

    sent, last = [], []

    def note(cps):
        for g in (Q, O):
            sent.extend(cps[g])
        return cps

    stream(tiles, wd_pair, bwd_down, 0, cut)
    back_b0 = give_back(B, 0)
    f0 = note(sums_begin(F, 0, back_f0, uo_f + up_f))
    stream(tiles, wd_pair, bwd_down, cut, tiles)
    back_b1 = give_back(B, 1)
    f1 = note(sums_begin(F, 1, back_f1, []))
    f0 = note(sums_relay(F, 0, f0))
    f1 = note(sums_relay(F, 1, f1))
    last += sums_end(F, 0, f0)
    b0 = note(sums_begin(B, 0, back_b0, uo_b + up_b))
    last += sums_end(F, 1, f1)
    b0 = note(sums_relay(B, 0, b0))
    b1 = note(sums_begin(B, 1, back_b1, []))
    last += sums_end(B, 0, b0)
    b1 = note(sums_relay(B, 1, b1))
    last += sums_end(B, 1, b1)

    wait_send(sent + back_f0[0] + back_f1[0] + back_b0[0] + back_b1[0])
    wait_send(n_f + np_f + n_b + np_b + s1_p + s2_o + s2_p)
    for cp in last:
        cp.wait()
    assert used[0] <= N_SEMS and used[1] <= N_LOCAL, used


def body(
    fwd_tokens,
    fwd_routes,
    fwd_gates,
    bwd_grads,
    bwd_routes,
    bwd_gates,
    saved_gate,
    saved_up,
    w_gate,
    w_up,
    w_down,
):
    tokens, grads = fwd_tokens[0], bwd_grads[0]
    width, inner = tokens.shape[1], w_gate.shape[3]
    quarter = width // 4
    any_, vmem = pl.BlockSpec(memory_space=pl.ANY), pl.BlockSpec(memory_space=pltpu.VMEM)

    def buf(*shape):
        return pltpu.VMEM(shape, BF16)

    scratch = (
        [buf(ROWS, width)] * 8
        + [buf(2 * ROWS, width)] * 2
        + [buf(2, 2, 4 * TAIL, quarter)] * 4
        + [buf(2, 2, TOK, width // 2)] * 2
        + [buf(2, 2, TOK, width)] * 2
        + [buf(2, TOK, width)]
        + [buf(2, 2, 4, 16, LANES)]
        + [buf(2, 4, 16, LANES)] * 3
        + [pltpu.VMEM((8, LANES), F32), pltpu.VMEM((8, TOK * 8), F32)]
        + [buf(ROWS, 2 * inner)] * 4
        + [buf(MAIN, 2 * inner), buf(2 * ROWS, 2 * inner)]
        + [buf(2, 4 * TAIL, inner // 2)] * 2
        + [buf(4 * TAIL, inner // 2)]
        + [buf(2, 4 * TAIL, inner // 2)] * 2
        + [buf(2 * ROWS, 2 * inner), buf(ROWS, TOK * 8), buf(2, 2, MAIN, ROWS), pltpu.VMEM((ROWS, LANES), F32)]
        + [buf(2, width, 256), buf(2, 256, width)]
        + [pltpu.SemaphoreType.DMA((N_SEMS,)), pltpu.SemaphoreType.DMA((N_SEMS,))]
        + [pltpu.SemaphoreType.DMA((N_LOCAL,)), pltpu.SemaphoreType.DMA((4, 2))]
    )
    out = jax.ShapeDtypeStruct(tokens.shape, BF16)
    rows = 2 * ROWS
    fo, fp, bo, bp = pl.pallas_call(
        kernel,
        out_shape=(out,) * 4,
        in_specs=[any_] * 7 + [vmem] * 6,
        out_specs=(any_,) * 4,
        scratch_shapes=scratch,
        compiler_params=pltpu.CompilerParams(
            collective_id=1, has_side_effects=True, vmem_limit_bytes=62 * 1024 * 1024
        ),
        cost_estimate=pl.CostEstimate(
            flops=12 * rows * width * inner, bytes_accessed=12 * width * inner, transcendentals=2 * rows * inner
        ),
    )(
        tokens,
        grads,
        saved_gate[0].reshape(-1, inner),
        saved_up[0].reshape(-1, inner),
        w_gate[0, 0],
        w_up[0, 0],
        w_down[0, 0],
        fwd_routes[0].T,
        fwd_gates[0].T,
        bwd_routes[0].T,
        bwd_gates[0].T,
        jnp.asarray(fold_matrix(), BF16),
        jnp.asarray(swap_matrix(), BF16),
    )
    next_inputs = (fo.astype(F32) + fp.astype(F32)).astype(BF16)
    prev_grads = (bo.astype(F32) + bp.astype(F32)).astype(BF16)
    return (next_inputs[None], prev_grads[None])


def solution(mesh):
    return jax.shard_map(
        body,
        mesh=mesh,
        in_specs=(P("section", "expert", None),) * 6 + (P("section", "expert", None, None),) * 5,
        out_specs=(P("section", "expert", None), P("section", "expert", None)),
        check_vma=False,
    )
```

```python
import functools

import jax
import jax.numpy as jnp
import numpy as np
from jax import lax
from jax.experimental import pallas as pl
from jax.experimental.pallas import tpu as pltpu
from jax.sharding import PartitionSpec as P

MESH = pl.DeviceIdType.MESH
F32 = jnp.float32
BF16 = jnp.bfloat16

RING = 4
CAP = 21
TOK = 80
GROUP = RING * CAP
EXTRA = GROUP - TOK
MAIN = RING * TOK
ROWS = RING * GROUP
TAIL = ROWS - MAIN
LANES = 128
N_SEMS = 192
N_LOCAL = 24


def row_of(block, place):
    return block * TOK + place if place < TOK else MAIN + block * EXTRA + place - TOK


def swap_matrix():
    m = np.zeros((ROWS, ROWS), np.float32)
    for q in range(RING):
        for t in range(RING):
            for i in range(CAP):
                m[row_of(t, q * CAP + i), row_of(q, t * CAP + i)] = 1
    return m


def fold_matrix():
    m = np.zeros((4 * TAIL, 4 * TAIL), np.float32)
    for a in range(4):
        for b in range(4):
            for j in range(4):
                m[b * 16 + a * 4 + j, a * 16 + b * 4 + j] = 1
    return m


def dot(a, b):
    return jnp.dot(a, b, preferred_element_type=F32)


def dot_t(a, b):
    return lax.dot_general(a, b, (((1,), (1,)), ((), ())), preferred_element_type=F32)


def aligned(i, size):
    return pl.ds(pl.multiple_of(i * size, size), size)


def kernel(
    tok_hbm,
    grd_hbm,
    sg_hbm,
    su_hbm,
    wg_hbm,
    wu_hbm,
    wd_hbm,
    routes_f, gates_f, routes_b, gates_b,
    fold,
    swap,
    out_fo, out_fp, out_bo, out_bp,
    g_fo, g_fp, g_bo, g_bp,
    pk_fo, pk_fp, pk_bo, pk_bp,
    x_f, x_b,
    es, er, ys, yr,
    ra, rb, rc, rd, zr,
    meta, mo, mz, mp, turn, spos,
    spk_o, spk_p, sg_o, sg_p, sz, sx,
    spe, sge, sze, s2e, sxe,
    hb, oh, ix, close, qm, gc, wa, wd_t,
    send, recv, local, wsem,
):
    e = lax.axis_index("expert")
    sec = lax.axis_index("section")
    n_sec = lax.axis_size("section")
    z, y, x = e // 16, lax.rem(e // 4, 4), lax.rem(e, 4)
    me = {"y": y, "x": x}
    width = tok_hbm.shape[1]
    inner = wg_hbm.shape[1]
    half = width // 2
    F, B, O, Q = 0, 1, 0, 1
    G = ((g_fo, g_fp), (g_bo, g_bp))
    PK = ((pk_fo, pk_fp), (pk_bo, pk_bp))
    X = (x_f, x_b)
    AG_AXIS = (("y", "x"), ("x", "y"))
    UNI_AXIS = (("x", "y"), ("y", "x"))
    CHUNKS = ((0, 2048), (2048, width - 2048))

    def at(axis, c):
        if axis == "y":
            return (sec, z * 16 + c * 4 + x)
        return (sec, z * 16 + y * 4 + c)

    def peer(axis, k):
        return at(axis, lax.rem(me[axis] + k, RING))

    other = (1 - z) * 16 + y * 4 + x
    partner = (sec, other)
    next_sec = lax.rem(sec + 1, n_sec)
    prev_sec = lax.rem(sec + n_sec - 1, n_sec)

    used = [0, 0]

    def remote(src, dst, device):
        i = used[0]
        used[0] += 1
        cp = pltpu.make_async_remote_copy(
            src_ref=src, dst_ref=dst, send_sem=send.at[i], recv_sem=recv.at[i],
            device_id=device, device_id_type=MESH,
        )
        cp.start()
        return cp

    def here(src, dst):
        i = used[1]
        used[1] += 1
        cp = pltpu.make_async_copy(src, dst, local.at[i])
        cp.start()
        return cp

    def wait_recv(cps):
        for cp in cps:
            cp.wait_recv()

    def wait_send(cps):
        for cp in cps:
            cp.wait_send()

    def turned(ref, fill):
        turn[...] = jnp.full((8, LANES), fill, F32)
        turn[:, 0:TOK] = ref[...].astype(F32)
        return turn[...]

    def places(f, routes, gates):
        named_by = turned(routes, -1.0)
        gate_by = turned(gates, 0.0)
        expert = lax.broadcasted_iota(jnp.int32, (32, LANES), 0).astype(F32)
        hot = [named_by[k : k + 1, :] == expert for k in range(8)]
        count = jnp.zeros((32, LANES), F32)
        gate = jnp.zeros((32, LANES), F32)
        for k in range(8):
            count += jnp.where(hot[k], 1.0, 0.0)
            gate += jnp.where(hot[k], gate_by[k : k + 1, :], 0.0)
        earlier = lax.broadcasted_iota(jnp.int32, (LANES, LANES), 0) < lax.broadcasted_iota(jnp.int32, (LANES, LANES), 1)
        within = dot(count.astype(BF16), jnp.where(earlier, 1.0, 0.0).astype(BF16))
        high = gate.astype(BF16).astype(F32)
        rows = jnp.concatenate([jnp.where(count > 0, within, -1.0), high, gate - high], axis=0).astype(BF16)
        r = lax.broadcasted_iota(jnp.int32, (64, 96), 0)
        message, kind, item = r // 16, lax.rem(r, 16) // 4, lax.rem(r, 4)
        col = lax.broadcasted_iota(jnp.int32, (64, 96), 1)
        for g in (O, Q):
            plane = z if g == O else 1 - z
            if AG_AXIS[f][g] == "y":
                index = plane * 16 + message * 4 + item
            else:
                index = plane * 16 + item * 4 + message
            pick = jnp.where(jnp.logical_and(kind < 3, col == kind * 32 + index), 1.0, 0.0).astype(BF16)
            got = dot(pick, rows).astype(BF16)
            for c in range(4):
                meta[f, g, c] = got[c * 16 : (c + 1) * 16, :]
        if f == F:
            return
        slot = jnp.concatenate(
            [jnp.sum(jnp.where(hot[k], within, 0.0), axis=0, keepdims=True) for k in range(8)], axis=0
        ).astype(jnp.int32)
        chosen = named_by.astype(jnp.int32)
        same = chosen // 16 == z
        cy, cx = lax.rem(chosen // 4, 4), lax.rem(chosen, 4)
        block = jnp.where(same, cx, cy)
        place = jnp.where(same, cy, cx) * CAP + slot
        row = jnp.where(place < TOK, block * TOK + place, MAIN + block * EXTRA + place - TOK)
        row = row + jnp.where(same, 0, ROWS)
        token = lax.broadcasted_iota(jnp.int32, (LANES, TOK * 8), 0)
        lane = lax.broadcasted_iota(jnp.int32, (LANES, TOK * 8), 1)
        spread = jnp.where(lane // 8 == token, 1.0, 0.0).astype(BF16)
        coarse = (row // 16).astype(F32).astype(BF16)
        fine = lax.rem(row, 16).astype(F32).astype(BF16)
        wide = 16.0 * dot(coarse, spread) + dot(fine, spread)
        mine = lax.broadcasted_iota(jnp.int32, (8, TOK * 8), 0) == lax.rem(lane[0:8, :], 8)
        total = jnp.sum(jnp.where(mine, wide, 0.0), axis=0, keepdims=True)
        spos[...] = jnp.broadcast_to(total, (8, TOK * 8))

    def wa_pair(j, slot):
        cols = pl.ds(pl.multiple_of(j * LANES, LANES), LANES)
        return (
            pltpu.make_async_copy(wg_hbm.at[:, cols], wa.at[slot, :, 0:LANES], wsem.at[0, slot]),
            pltpu.make_async_copy(wu_hbm.at[:, cols], wa.at[slot, :, LANES : 2 * LANES], wsem.at[1, slot]),
        )

    def wa_down(j, slot):
        cols = pl.ds(pl.multiple_of(j * 256, 256), 256)
        return (pltpu.make_async_copy(wd_hbm.at[:, cols], wa.at[slot, 0:inner, :], wsem.at[0, slot]),)

    def wd_rows(j, slot):
        rows = aligned(j, 256)
        return (pltpu.make_async_copy(wd_hbm.at[rows, :], wd_t.at[slot], wsem.at[2, slot]),)

    def wd_pair(j, slot):
        rows = aligned(j, 256)
        return (
            pltpu.make_async_copy(wg_hbm.at[rows, :], wd_t.at[slot, :, 0:inner], wsem.at[2, slot]),
            pltpu.make_async_copy(wu_hbm.at[rows, :], wd_t.at[slot, :, inner : 2 * inner], wsem.at[3, slot]),
        )

    def begin(tiles):
        for cp in tiles(0, 0):
            cp.start()

    def stream(n, tiles, work, first=0, last=None):
        def step(j, carry):
            slot = lax.rem(j, 2)

            @pl.when(j + 1 < n)
            def _():
                for cp in tiles(j + 1, 1 - slot):
                    cp.start()

            for cp in tiles(j, slot):
                cp.wait()
            work(j, slot)
            return carry

        lax.fori_loop(first, n if last is None else last, step, 0)

    def fold_out(src, row0, dst, col0=0, size=None):
        w4 = (src.shape[1] if size is None else size) // 4
        a = jnp.concatenate(
            [src[row0 : row0 + TAIL, col0 + c * w4 : col0 + (c + 1) * w4] for c in range(4)], axis=0)
        dst[...] = dot(fold[...], a).astype(BF16)

    def fold_in(src, dst, row0, col0=0, size=None):
        w4 = (dst.shape[1] if size is None else size) // 4
        a = dot(fold[...], src[...]).astype(BF16)
        for c in range(4):
            dst[row0 : row0 + TAIL, col0 + c * w4 : col0 + (c + 1) * w4] = a[c * TAIL : (c + 1) * TAIL, :]

    def exchange(axis, src, src_off, src_extra, dst, dst_off, dst_extra, cols=slice(None)):
        cps, own_copy = exchange_main(axis, src, src_off, dst, dst_off, cols)
        return cps + exchange_extra(axis, src_extra, dst_extra), own_copy

    def exchange_main(axis, src, src_off, dst, dst_off, cols=slice(None)):
        m = me[axis]
        cps = []
        for k in (2, 1, 3):
            c = lax.rem(m + k, RING)
            cps.append(remote(
                src.at[pl.ds(pl.multiple_of(src_off + c * TOK, 16), TOK), cols],
                dst.at[pl.ds(pl.multiple_of(dst_off + m * TOK, 16), TOK), cols],
                at(axis, c)))
        own_copy = here(
            src.at[pl.ds(pl.multiple_of(src_off + m * TOK, 16), TOK), cols],
            dst.at[pl.ds(pl.multiple_of(dst_off + m * TOK, 16), TOK), cols])
        return cps, own_copy

    def exchange_extra(axis, src_extra, dst_extra):
        m = me[axis]
        cps = []
        for k in (2, 1, 3):
            c = lax.rem(m + k, RING)
            cps.append(remote(src_extra.at[aligned(c, TAIL), :], dst_extra.at[aligned(m, TAIL), :], at(axis, c)))
        dst_extra[aligned(m, TAIL), :] = src_extra[aligned(m, TAIL), :]
        return cps

    def slot_of(ref, c, cols=None):
        rows = pl.ds(pl.multiple_of(c * TOK, 16), TOK)
        return ref.at[rows, :] if cols is None else ref.at[rows, cols]

    LO, HI = pl.ds(0, half), pl.ds(half, half)

    def gather_begin(axis, ref, cols):
        m = me[axis]
        return [remote(slot_of(ref, m, cols), slot_of(ref, m, cols), peer(axis, k))
                for k in ((1, 3) if cols is LO else (3, 1))]

    def gather_relay(axis, ref, low, high):
        m = me[axis]
        before, after = lax.rem(m + 3, RING), lax.rem(m + 1, RING)
        low[0].wait_recv()
        a = remote(slot_of(ref, before, LO), slot_of(ref, before, LO), peer(axis, 1))
        high[0].wait_recv()
        b = remote(slot_of(ref, after, HI), slot_of(ref, after, HI), peer(axis, 3))
        return [a, b, low[1], high[1]]

    def pack_index(f, g, notes):
        wait_recv(notes)
        wide = lax.broadcasted_iota(jnp.int32, (TOK, LANES), 0).astype(F32)
        tail = lax.broadcasted_iota(jnp.int32, (TAIL, LANES), 0)
        tail_place = (TOK + lax.rem(tail, EXTRA)).astype(F32)
        tail_block = tail // EXTRA
        metas = (mo, mp)[g]
        gate = [jnp.zeros((TOK, 1), F32)] * RING
        tail_gate = jnp.zeros((TAIL, 1), F32)
        for q in range(RING):
            m = metas[f, q].astype(F32)
            s = jnp.where(m >= 0, m + q * CAP, -1.0)
            w = m[4:8, :] + m[8:12, :]
            cols = slice(q * LANES, (q + 1) * LANES)
            chosen = jnp.zeros((TAIL, LANES), F32)
            weight = jnp.zeros((TAIL, LANES), F32)
            for t in range(RING):
                row, w_row = s[t : t + 1, :], w[t : t + 1, :]
                hit = wide == row
                oh[t * TOK : (t + 1) * TOK, cols] = jnp.where(hit, 1.0, 0.0).astype(BF16)
                chosen = jnp.where(tail_block == t, row, chosen)
                if f == B:
                    gate[t] += jnp.sum(jnp.where(hit, w_row, 0.0), axis=1, keepdims=True)
                    weight = jnp.where(tail_block == t, w_row, weight)
            hit = chosen == tail_place
            oh[MAIN:ROWS, cols] = jnp.where(hit, 1.0, 0.0).astype(BF16)
            tail_gate += jnp.sum(jnp.where(hit, weight, 0.0), axis=1, keepdims=True)
        if f == B:
            for t in range(RING):
                gc[g, t * TOK : (t + 1) * TOK, :] = jnp.broadcast_to(gate[t], (TOK, LANES))
            gc[g, MAIN:ROWS, :] = jnp.broadcast_to(tail_gate, (TAIL, LANES))

        ix[f, g] = dot(oh[:, 0 : RING * LANES], close[...]).astype(BF16)

    def pack_rows(f, g):
        def cols_step(j, carry):
            cols = aligned(j, 512)
            acc = dot(ix[f, g], G[f][g][0:MAIN, cols])
            if f == B:
                acc = acc * gc[g, :, 0:1]
            PK[f][g][:, cols] = acc.astype(BF16)
            return carry

        lax.fori_loop(0, width // 512, cols_step, 0)
        fold_out(PK[f][g], MAIN, es.at[f, g])

    def weights(f, g):
        lane = lax.broadcasted_iota(jnp.int32, (TOK, ROWS), 1)
        in_main = lane < MAIN
        block = jnp.where(in_main, lane // TOK, (lane - MAIN) // EXTRA)
        place = jnp.where(in_main, lax.rem(lane, TOK), TOK + lax.rem(lane - MAIN, EXTRA)).astype(F32)
        metas = (mo, mp)[g]
        for q in range(RING):
            m = jnp.concatenate([metas[f, q].astype(F32), jnp.zeros((LANES - 16, LANES), F32)], axis=0)
            m = m.T[0:TOK, :]
            s = m[:, 0:1]
            w = m[:, 4:5]
            for t in range(1, RING):
                s = jnp.where(block == t, m[:, t : t + 1], s)
                w = jnp.where(block == t, m[:, 4 + t : 5 + t], w)
            hit = jnp.logical_and(s >= 0, s + q * CAP == place)
            qm[f, g, q * TOK : (q + 1) * TOK, :] = jnp.where(hit, w if f == F else 1.0, 0.0).astype(BF16)

    def combine(f, g, h):
        col0, size = CHUNKS[h]
        fold_in(yr.at[f, g, :, pl.ds(col0 // 4, size // 4)], G[f][g], MAIN, col0, size)

        def cols_step(j, carry):
            cols = aligned(j, 512)
            PK[f][g][0:MAIN, cols] = dot(qm[f, g], G[f][g][:, cols]).astype(BF16)
            return carry

        lax.fori_loop(col0 // 512, (col0 + size) // 512, cols_step, 0)

    def parts(h):
        col0, size = CHUNKS[h]
        return (pl.ds(col0, size // 2), pl.ds(col0 + size // 2, size // 2)), pl.ds(col0 // 2, size // 2), pl.ds(col0, size)

    def scatter_begin(f, g, h):
        axis, ref = AG_AXIS[f][g], PK[f][g]
        (lo, hi), short, _ = parts(h)
        far = lax.rem(me[axis] + 2, RING)
        return [remote(slot_of(ref, far, lo), ra.at[f, g, :, short], peer(axis, 1)),
                remote(slot_of(ref, far, hi), rb.at[f, g, :, short], peer(axis, 3))]

    def scatter_relay(f, g, h, first):
        axis, ref = AG_AXIS[f][g], PK[f][g]
        ends, short, whole = parts(h)
        m = me[axis]
        cps = []
        for i, (k, got, dst) in enumerate(((1, ra, rc), (3, rb, rd))):
            first[i].wait_recv()
            c = lax.rem(m + k, RING)
            rows = pl.ds(pl.multiple_of(c * TOK, 16), TOK)
            ref[rows, ends[i]] = (ref[rows, ends[i]].astype(F32) + got[f, g, :, short].astype(F32)).astype(BF16)
            cps.append(remote(slot_of(ref, c, whole), dst.at[f, g, :, whole], peer(axis, k)))
        return cps

    def scatter_end(f, g, h, cps, out, device):
        axis, ref = AG_AXIS[f][g], PK[f][g]
        col0, size = CHUNKS[h]
        wait_recv(cps)
        rows = pl.ds(pl.multiple_of(me[axis] * TOK, 16), TOK)

        def cols_step(j, carry):
            cols = aligned(j, 512)
            acc = ref[rows, cols].astype(F32) + rc[f, g, :, cols].astype(F32) + rd[f, g, :, cols].astype(F32)
            ref[rows, cols] = acc.astype(BF16)
            return carry

        lax.fori_loop(col0 // 512, (col0 + size) // 512, cols_step, 0)
        whole = pl.ds(col0, size)
        return remote(slot_of(ref, me[axis], whole), out.at[:, whole], device)

    own = [here(tok_hbm, slot_of(g_fo, y)), here(grd_hbm, slot_of(g_bo, x))]
    saved_in = [here(sg_hbm, hb.at[0 : TOK * 8, 0:inner]), here(su_hbm, hb.at[0 : TOK * 8, inner : 2 * inner])]
    begin(wa_pair)
    begin(wd_rows)

    barrier = pltpu.get_barrier_semaphore()
    everyone = [partner, (next_sec, e), (prev_sec, e), (next_sec, other), (prev_sec, other)]
    everyone += [peer(a, k) for a in ("y", "x") for k in (1, 2, 3)]
    for device in everyone:
        pl.semaphore_signal(barrier, inc=1, device_id=device, device_id_type=MESH)
    c = lax.broadcasted_iota(jnp.int32, close.shape, 0)
    j = lax.broadcasted_iota(jnp.int32, close.shape, 1)
    same = jnp.logical_and(c // LANES == j // TOK, lax.rem(c, LANES) == lax.rem(j, TOK))
    close[...] = jnp.where(same, 1.0, 0.0).astype(BF16)
    pl.semaphore_wait(barrier, len(everyone))

    def partner_send(f, cols):
        return remote(
            slot_of(G[f][O], me[AG_AXIS[f][O]], cols), slot_of(G[f][Q], me[AG_AXIS[f][Q]], cols), partner)

    def notes_begin(f):
        axis = AG_AXIS[f][O]
        m = me[axis]
        notes = [remote(meta.at[f, Q], mz.at[f], partner)]
        for k in (1, 2, 3):
            c = lax.rem(m + k, RING)
            notes.append(remote(meta.at[f, O, c], mo.at[f, m], at(axis, c)))
        mo[f, m] = meta[f, O, m]
        return notes

    def partner_notes(f, notes):
        axis = AG_AXIS[f][Q]
        m = me[axis]
        notes[0].wait_recv()
        more = []
        for k in (1, 2, 3):
            c = lax.rem(m + k, RING)
            more.append(remote(mz.at[f, c], mp.at[f, m], at(axis, c)))
        mp[f, m] = mz[f, m]
        return more

    def partner_begin(f, to_z, cols):
        to_z.wait_recv()
        return gather_begin(AG_AXIS[f][Q], G[f][Q], cols)

    def packed(f, g, relays):
        wait_recv(relays)
        pack_rows(f, g)
        return exchange_main(UNI_AXIS[f][g], PK[f][g], 0, X[f], g * ROWS)

    def packed_extra(f, g, sent, relays):
        wait_send(sent + relays[0:2])
        return exchange_extra(UNI_AXIS[f][g], es.at[f, g], er.at[f, g])

    def saved_pack(g, dst):
        index = (lax.broadcasted_iota(jnp.int32, (ROWS, TOK * 8), 0) + g * ROWS).astype(F32)
        oh[...] = jnp.where(spos[0:1, :] == index, 1.0, 0.0).astype(BF16)

        def cols_step(j, carry):
            cols = aligned(j, 512)
            dst[:, cols] = dot(oh[...], hb[0 : TOK * 8, cols]).astype(BF16)
            return carry

        lax.fori_loop(0, 2 * inner // 512, cols_step, 0)
        fold_out(dst, MAIN, spe.at[g])

    own[F].wait()
    of_l = gather_begin("y", g_fo, LO)
    zf_l = partner_send(F, LO)
    of_h = gather_begin("y", g_fo, HI)
    own[B].wait()
    ob_l = gather_begin("x", g_bo, LO)
    zb_l = partner_send(B, LO)
    ob_h = gather_begin("x", g_bo, HI)
    places(F, routes_f, gates_f)
    n_f = notes_begin(F)
    places(B, routes_b, gates_b)
    n_b = notes_begin(B)
    ro_f = gather_relay("y", g_fo, of_l, of_h)
    ro_b = gather_relay("x", g_bo, ob_l, ob_h)
    pf_l = partner_begin(F, zf_l, LO)
    pb_l = partner_begin(B, zb_l, LO)
    zf_h = partner_send(F, HI)
    zb_h = partner_send(B, HI)
    pack_index(F, O, n_f[1:])
    pack_index(B, O, n_b[1:])
    for cp in saved_in:
        cp.wait()
    saved_pack(Q, spk_p)
    uo_f, lo_f = packed(F, O, ro_f)
    uo_b, lo_b = packed(B, O, ro_b)
    pf_h = partner_begin(F, zf_h, HI)
    pb_h = partner_begin(B, zb_h, HI)
    s1_z = [remote(spk_p.at[0:MAIN, :], sz, partner), remote(spe.at[1], sze, partner)]
    np_f = partner_notes(F, n_f)
    np_b = partner_notes(B, n_b)
    uo_f += packed_extra(F, O, [zf_l, zf_h] + of_l + of_h, ro_f)
    uo_b += packed_extra(B, O, [zb_l, zb_h] + ob_l + ob_h, ro_b)
    rp_f = gather_relay("x", g_fp, pf_l, pf_h)
    rp_b = gather_relay("y", g_bp, pb_l, pb_h)
    pack_index(F, Q, np_f)
    pack_index(B, Q, np_b)
    saved_pack(O, spk_o)
    up_f, lp_f = packed(F, Q, rp_f)
    up_f += packed_extra(F, Q, pf_l + pf_h, rp_f)
    s1_o, sl_o = exchange("x", spk_o, 0, spe.at[0], sg_o, 0, sge.at[0])
    up_b, lp_b = packed(B, Q, rp_b)
    up_b += packed_extra(B, Q, pb_l + pb_h, rp_b)
    weights(F, O)
    weights(F, Q)
    wait_recv(s1_z)
    s1_p, sl_p = exchange("y", sz, 0, sze, sg_p, 0, sge.at[1])

    def saved_second(g, first, own_copy, before, got, out):
        wait_recv(first)
        own_copy.wait()
        wait_send(before)
        fold_in(sge.at[g], got, MAIN)

        def cols_step(j, carry):
            cols = aligned(j, 512)
            out[:, cols] = dot(swap[...], got[:, cols]).astype(BF16)
            return carry

        lax.fori_loop(0, 2 * inner // 512, cols_step, 0)
        fold_out(out, MAIN, s2e.at[g])
        return exchange(UNI_AXIS[B][g], out, 0, s2e.at[g], sx, g * ROWS, sxe.at[g])

    weights(B, O)
    weights(B, Q)

    wait_recv(uo_f + up_f)
    lo_f.wait()
    lp_f.wait()
    for g in (O, Q):
        fold_in(er.at[F, g], x_f, g * ROWS + MAIN)

    def fwd_hidden(j, slot):
        for r in range(2):
            rows = slice(r * ROWS, (r + 1) * ROWS)
            both = dot(x_f[rows, :], wa[slot])
            gate, up = both[:, 0:LANES], both[:, LANES : 2 * LANES]
            hb[rows, aligned(j, LANES)] = (gate / (1.0 + jnp.exp(-gate)) * up).astype(BF16)

    stream(inner // LANES, wa_pair, fwd_hidden)
    begin(wa_down)
    s2_o, sm_o = saved_second(O, s1_o, sl_o, s1_o, sg_o, spk_o)
    s2_p, sm_p = saved_second(Q, s1_p, sl_p, s1_z, sg_p, spk_p)

    def fwd_down(j, slot):
        for r in range(2):
            rows = slice(r * ROWS, (r + 1) * ROWS)
            x_f[rows, aligned(j, 256)] = dot(hb[rows, 0:inner], wa[slot, 0:inner, :]).astype(BF16)

    def give_back(f, h):
        col0, size = CHUNKS[h]
        cps, owns = [], []
        for g in (Q, O):
            extra = (f, g, slice(None), pl.ds(col0 // 4, size // 4))
            fold_out(X[f], g * ROWS + MAIN, ys.at[extra], col0, size)
            c, o = exchange(
                UNI_AXIS[f][g], X[f], g * ROWS, ys.at[extra], G[f][g], 0, yr.at[extra], pl.ds(col0, size))
            cps = cps + c
            owns.append(o)
        return cps, owns

    tiles = width // 256
    cut = CHUNKS[0][1] // 256
    stream(tiles, wa_down, fwd_down, 0, cut)
    back_f0 = give_back(F, 0)
    stream(tiles, wa_down, fwd_down, cut, tiles)
    back_f1 = give_back(F, 1)

    wait_recv(uo_b + up_b + s2_o + s2_p)
    for cp in (lo_b, lp_b, sm_o, sm_p):
        cp.wait()
    for g in (O, Q):
        fold_in(er.at[B, g], x_b, g * ROWS + MAIN)
        fold_in(sxe.at[g], sx, g * ROWS + MAIN)

    def bwd_hidden(j, slot):
        cols, more = aligned(j, 256), pl.ds(pl.multiple_of(inner + j * 256, 256), 256)
        for r in range(2):
            rows = slice(r * ROWS, (r + 1) * ROWS)
            grad = dot_t(x_b[rows, :], wd_t[slot])
            a = sx[rows, cols].astype(F32)
            b = sx[rows, more].astype(F32)
            s = 1.0 / (1.0 + jnp.exp(-a))
            hb[rows, cols] = (grad * b * s * (1.0 + a * (1.0 - s))).astype(BF16)
            hb[rows, more] = (grad * a * s).astype(BF16)

    stream(inner // 256, wd_rows, bwd_hidden)
    begin(wd_pair)

    def bwd_down(j, slot):
        for r in range(2):
            rows = slice(r * ROWS, (r + 1) * ROWS)
            x_b[rows, aligned(j, 256)] = dot_t(hb[rows, :], wd_t[slot, :, 0 : 2 * inner]).astype(BF16)

    def sums_begin(f, h, back, before):
        cps, owns = back
        wait_recv(cps)
        for cp in owns:
            cp.wait()
        wait_send(before)
        first = {}
        for g in (Q, O):
            combine(f, g, h)
            first[g] = scatter_begin(f, g, h)
        return first

    def sums_relay(f, h, first):
        return {g: scatter_relay(f, g, h, first[g]) for g in (Q, O)}

    outs = ((out_fo, out_fp), (out_bo, out_bp))
    to_sec = (next_sec, prev_sec)

    def sums_end(f, h, second):
        return [scatter_end(f, g, h, second[g], outs[f][g], (to_sec[f], (e, other)[g])) for g in (Q, O)]

    sent, last = [], []

    def note(cps):
        for g in (Q, O):
            sent.extend(cps[g])
        return cps

    stream(tiles, wd_pair, bwd_down, 0, cut)
    back_b0 = give_back(B, 0)
    f0 = note(sums_begin(F, 0, back_f0, uo_f + up_f))
    stream(tiles, wd_pair, bwd_down, cut, tiles)
    back_b1 = give_back(B, 1)
    f1 = note(sums_begin(F, 1, back_f1, []))
    f0 = note(sums_relay(F, 0, f0))
    f1 = note(sums_relay(F, 1, f1))
    last += sums_end(F, 0, f0)
    b0 = note(sums_begin(B, 0, back_b0, uo_b + up_b))
    last += sums_end(F, 1, f1)
    b0 = note(sums_relay(B, 0, b0))
    b1 = note(sums_begin(B, 1, back_b1, []))
    last += sums_end(B, 0, b0)
    b1 = note(sums_relay(B, 1, b1))
    last += sums_end(B, 1, b1)

    wait_send(sent + back_f0[0] + back_f1[0] + back_b0[0] + back_b1[0])
    wait_send(n_f + np_f + n_b + np_b + s1_p + s2_o + s2_p)
    for cp in last:
        cp.wait()
    assert used[0] <= N_SEMS and used[1] <= N_LOCAL, used


def body(
    fwd_tokens,
    fwd_routes,
    fwd_gates,
    bwd_grads,
    bwd_routes,
    bwd_gates,
    saved_gate,
    saved_up,
    w_gate,
    w_up,
    w_down,
):
    tokens, grads = fwd_tokens[0], bwd_grads[0]
    width, inner = tokens.shape[1], w_gate.shape[3]
    quarter = width // 4
    any_, vmem = pl.BlockSpec(memory_space=pl.ANY), pl.BlockSpec(memory_space=pltpu.VMEM)

    def buf(*shape):
        return pltpu.VMEM(shape, BF16)

    scratch = (
        [buf(ROWS, width)] * 8
        + [buf(2 * ROWS, width)] * 2
        + [buf(2, 2, 4 * TAIL, quarter)] * 4
        + [buf(2, 2, TOK, width // 2)] * 2
        + [buf(2, 2, TOK, width)] * 2
        + [buf(2, TOK, width)]
        + [buf(2, 2, 4, 16, LANES)]
        + [buf(2, 4, 16, LANES)] * 3
        + [pltpu.VMEM((8, LANES), F32), pltpu.VMEM((8, TOK * 8), F32)]
        + [buf(ROWS, 2 * inner)] * 4
        + [buf(MAIN, 2 * inner), buf(2 * ROWS, 2 * inner)]
        + [buf(2, 4 * TAIL, inner // 2)] * 2
        + [buf(4 * TAIL, inner // 2)]
        + [buf(2, 4 * TAIL, inner // 2)] * 2
        + [buf(2 * ROWS, 2 * inner), buf(ROWS, TOK * 8), buf(2, 2, ROWS, MAIN), buf(RING * LANES, MAIN), buf(2, 2, MAIN, ROWS)]
        + [pltpu.VMEM((2, ROWS, LANES), F32)]
        + [buf(2, width, 256), buf(2, 256, width)]
        + [pltpu.SemaphoreType.DMA((N_SEMS,)), pltpu.SemaphoreType.DMA((N_SEMS,))]
        + [pltpu.SemaphoreType.DMA((N_LOCAL,)), pltpu.SemaphoreType.DMA((4, 2))]
    )
    out = jax.ShapeDtypeStruct(tokens.shape, BF16)
    rows = 2 * ROWS
    fo, fp, bo, bp = pl.pallas_call(
        kernel,
        out_shape=(out,) * 4,
        in_specs=[any_] * 7 + [vmem] * 6,
        out_specs=(any_,) * 4,
        scratch_shapes=scratch,
        compiler_params=pltpu.CompilerParams(
            collective_id=1, has_side_effects=True, vmem_limit_bytes=62 * 1024 * 1024
        ),
        cost_estimate=pl.CostEstimate(
            flops=12 * rows * width * inner, bytes_accessed=12 * width * inner, transcendentals=2 * rows * inner
        ),
    )(
        tokens,
        grads,
        saved_gate[0].reshape(-1, inner),
        saved_up[0].reshape(-1, inner),
        w_gate[0, 0],
        w_up[0, 0],
        w_down[0, 0],
        fwd_routes[0].T,
        fwd_gates[0].T,
        bwd_routes[0].T,
        bwd_gates[0].T,
        jnp.asarray(fold_matrix(), BF16),
        jnp.asarray(swap_matrix(), BF16),
    )
    next_inputs = (fo.astype(F32) + fp.astype(F32)).astype(BF16)
    prev_grads = (bo.astype(F32) + bp.astype(F32)).astype(BF16)
    return (next_inputs[None], prev_grads[None])


def solution(mesh):
    return jax.shard_map(
        body,
        mesh=mesh,
        in_specs=(P("section", "expert", None),) * 6 + (P("section", "expert", None, None),) * 5,
        out_specs=(P("section", "expert", None), P("section", "expert", None)),
        check_vma=False,
    )
```

```python
import functools

import jax
import jax.numpy as jnp
import numpy as np
from jax import lax
from jax.experimental import pallas as pl
from jax.experimental.pallas import tpu as pltpu
from jax.sharding import PartitionSpec as P

MESH = pl.DeviceIdType.MESH
F32 = jnp.float32
BF16 = jnp.bfloat16

RING = 4
CAP = 21
TOK = 80
GROUP = RING * CAP
EXTRA = GROUP - TOK
MAIN = RING * TOK
ROWS = RING * GROUP
TAIL = ROWS - MAIN
LANES = 128
N_SEMS = 192
N_LOCAL = 24


def row_of(block, place):
    return block * TOK + place if place < TOK else MAIN + block * EXTRA + place - TOK


def swap_matrix():
    m = np.zeros((ROWS, ROWS), np.float32)
    for q in range(RING):
        for t in range(RING):
            for i in range(CAP):
                m[row_of(t, q * CAP + i), row_of(q, t * CAP + i)] = 1
    return m


def fold_matrix():
    m = np.zeros((4 * TAIL, 4 * TAIL), np.float32)
    for a in range(4):
        for b in range(4):
            for j in range(4):
                m[b * 16 + a * 4 + j, a * 16 + b * 4 + j] = 1
    return m


def dot(a, b):
    return jnp.dot(a, b, preferred_element_type=F32)


def dot_t(a, b):
    return lax.dot_general(a, b, (((1,), (1,)), ((), ())), preferred_element_type=F32)


def aligned(i, size):
    return pl.ds(pl.multiple_of(i * size, size), size)


def kernel(
    tok_hbm,
    grd_hbm,
    sg_hbm,
    su_hbm,
    wg_hbm,
    wu_hbm,
    wd_hbm,
    routes_f, gates_f, routes_b, gates_b,
    fold,
    swap,
    out_fo, out_fp, out_bo, out_bp,
    g_fo, g_fp, g_bo, g_bp,
    pk_fo, pk_fp, pk_bo, pk_bp,
    x_f, x_b,
    es, er, ys, yr,
    ra, rb, rc, rd, zr,
    meta, mo, mz, mp, turn, spos,
    spk_o, spk_p, sg_o, sg_p, sz, sx,
    spe, sge, sze, s2e, sxe,
    hb, oh, ix, close, qm, gc, wa, wd_t,
    send, recv, local, wsem,
):
    e = lax.axis_index("expert")
    sec = lax.axis_index("section")
    n_sec = lax.axis_size("section")
    z, y, x = e // 16, lax.rem(e // 4, 4), lax.rem(e, 4)
    me = {"y": y, "x": x}
    width = tok_hbm.shape[1]
    inner = wg_hbm.shape[1]
    half = width // 2
    F, B, O, Q = 0, 1, 0, 1
    G = ((g_fo, g_fp), (g_bo, g_bp))
    PK = ((pk_fo, pk_fp), (pk_bo, pk_bp))
    X = (x_f, x_b)
    AG_AXIS = (("y", "x"), ("x", "y"))
    UNI_AXIS = (("x", "y"), ("y", "x"))
    CHUNKS = ((0, 2048), (2048, width - 2048))

    def at(axis, c):
        if axis == "y":
            return (sec, z * 16 + c * 4 + x)
        return (sec, z * 16 + y * 4 + c)

    def peer(axis, k):
        return at(axis, lax.rem(me[axis] + k, RING))

    other = (1 - z) * 16 + y * 4 + x
    partner = (sec, other)
    next_sec = lax.rem(sec + 1, n_sec)
    prev_sec = lax.rem(sec + n_sec - 1, n_sec)

    used = [0, 0]

    def remote(src, dst, device):
        i = used[0]
        used[0] += 1
        cp = pltpu.make_async_remote_copy(
            src_ref=src, dst_ref=dst, send_sem=send.at[i], recv_sem=recv.at[i],
            device_id=device, device_id_type=MESH,
        )
        cp.start()
        return cp

    def here(src, dst):
        i = used[1]
        used[1] += 1
        cp = pltpu.make_async_copy(src, dst, local.at[i])
        cp.start()
        return cp

    def wait_recv(cps):
        for cp in cps:
            cp.wait_recv()

    def wait_send(cps):
        for cp in cps:
            cp.wait_send()

    def turned(ref, fill):
        turn[...] = jnp.full((8, LANES), fill, F32)
        turn[:, 0:TOK] = ref[...].astype(F32)
        return turn[...]

    def places(f, routes, gates):
        named_by = turned(routes, -1.0)
        gate_by = turned(gates, 0.0)
        expert = lax.broadcasted_iota(jnp.int32, (32, LANES), 0).astype(F32)
        hot = [named_by[k : k + 1, :] == expert for k in range(8)]
        count = jnp.zeros((32, LANES), F32)
        gate = jnp.zeros((32, LANES), F32)
        for k in range(8):
            count += jnp.where(hot[k], 1.0, 0.0)
            gate += jnp.where(hot[k], gate_by[k : k + 1, :], 0.0)
        earlier = lax.broadcasted_iota(jnp.int32, (LANES, LANES), 0) < lax.broadcasted_iota(jnp.int32, (LANES, LANES), 1)
        within = dot(count.astype(BF16), jnp.where(earlier, 1.0, 0.0).astype(BF16))
        high = gate.astype(BF16).astype(F32)
        rows = jnp.concatenate([jnp.where(count > 0, within, -1.0), high, gate - high], axis=0).astype(BF16)
        r = lax.broadcasted_iota(jnp.int32, (64, 96), 0)
        message, kind, item = r // 16, lax.rem(r, 16) // 4, lax.rem(r, 4)
        col = lax.broadcasted_iota(jnp.int32, (64, 96), 1)
        for g in (O, Q):
            plane = z if g == O else 1 - z
            if AG_AXIS[f][g] == "y":
                index = plane * 16 + message * 4 + item
            else:
                index = plane * 16 + item * 4 + message
            pick = jnp.where(jnp.logical_and(kind < 3, col == kind * 32 + index), 1.0, 0.0).astype(BF16)
            got = dot(pick, rows).astype(BF16)
            for c in range(4):
                meta[f, g, c] = got[c * 16 : (c + 1) * 16, :]
        if f == F:
            return
        slot = jnp.concatenate(
            [jnp.sum(jnp.where(hot[k], within, 0.0), axis=0, keepdims=True) for k in range(8)], axis=0
        ).astype(jnp.int32)
        chosen = named_by.astype(jnp.int32)
        same = chosen // 16 == z
        cy, cx = lax.rem(chosen // 4, 4), lax.rem(chosen, 4)
        block = jnp.where(same, cx, cy)
        place = jnp.where(same, cy, cx) * CAP + slot
        row = jnp.where(place < TOK, block * TOK + place, MAIN + block * EXTRA + place - TOK)
        row = row + jnp.where(same, 0, ROWS)
        token = lax.broadcasted_iota(jnp.int32, (LANES, TOK * 8), 0)
        lane = lax.broadcasted_iota(jnp.int32, (LANES, TOK * 8), 1)
        spread = jnp.where(lane // 8 == token, 1.0, 0.0).astype(BF16)
        coarse = (row // 16).astype(F32).astype(BF16)
        fine = lax.rem(row, 16).astype(F32).astype(BF16)
        wide = 16.0 * dot(coarse, spread) + dot(fine, spread)
        mine = lax.broadcasted_iota(jnp.int32, (8, TOK * 8), 0) == lax.rem(lane[0:8, :], 8)
        total = jnp.sum(jnp.where(mine, wide, 0.0), axis=0, keepdims=True)
        spos[...] = jnp.broadcast_to(total, (8, TOK * 8))

    def wa_pair(j, slot):
        cols = pl.ds(pl.multiple_of(j * LANES, LANES), LANES)
        return (
            pltpu.make_async_copy(wg_hbm.at[:, cols], wa.at[slot, :, 0:LANES], wsem.at[0, slot]),
            pltpu.make_async_copy(wu_hbm.at[:, cols], wa.at[slot, :, LANES : 2 * LANES], wsem.at[1, slot]),
        )

    def wa_down(j, slot):
        cols = pl.ds(pl.multiple_of(j * 256, 256), 256)
        return (pltpu.make_async_copy(wd_hbm.at[:, cols], wa.at[slot, 0:inner, :], wsem.at[0, slot]),)

    def wd_rows(j, slot):
        rows = aligned(j, 256)
        return (pltpu.make_async_copy(wd_hbm.at[rows, :], wd_t.at[slot], wsem.at[2, slot]),)

    def wd_pair(j, slot):
        rows = aligned(j, 256)
        return (
            pltpu.make_async_copy(wg_hbm.at[rows, :], wd_t.at[slot, :, 0:inner], wsem.at[2, slot]),
            pltpu.make_async_copy(wu_hbm.at[rows, :], wd_t.at[slot, :, inner : 2 * inner], wsem.at[3, slot]),
        )

    def begin(tiles):
        for cp in tiles(0, 0):
            cp.start()

    def stream(n, tiles, work, first=0, last=None):
        def step(j, carry):
            slot = lax.rem(j, 2)

            @pl.when(j + 1 < n)
            def _():
                for cp in tiles(j + 1, 1 - slot):
                    cp.start()

            for cp in tiles(j, slot):
                cp.wait()
            work(j, slot)
            return carry

        lax.fori_loop(first, n if last is None else last, step, 0)

    def fold_out(src, row0, dst, col0=0, size=None):
        w4 = (src.shape[1] if size is None else size) // 4
        a = jnp.concatenate(
            [src[row0 : row0 + TAIL, col0 + c * w4 : col0 + (c + 1) * w4] for c in range(4)], axis=0)
        dst[...] = dot(fold[...], a).astype(BF16)

    def fold_in(src, dst, row0, col0=0, size=None):
        w4 = (dst.shape[1] if size is None else size) // 4
        a = dot(fold[...], src[...]).astype(BF16)
        for c in range(4):
            dst[row0 : row0 + TAIL, col0 + c * w4 : col0 + (c + 1) * w4] = a[c * TAIL : (c + 1) * TAIL, :]

    def exchange(axis, src, src_off, src_extra, dst, dst_off, dst_extra, cols=slice(None)):
        cps, own_copy = exchange_main(axis, src, src_off, dst, dst_off, cols)
        return cps + exchange_extra(axis, src_extra, dst_extra), own_copy

    def exchange_main(axis, src, src_off, dst, dst_off, cols=slice(None)):
        m = me[axis]
        cps = []
        for k in (2, 1, 3):
            c = lax.rem(m + k, RING)
            cps.append(remote(
                src.at[pl.ds(pl.multiple_of(src_off + c * TOK, 16), TOK), cols],
                dst.at[pl.ds(pl.multiple_of(dst_off + m * TOK, 16), TOK), cols],
                at(axis, c)))
        own_copy = here(
            src.at[pl.ds(pl.multiple_of(src_off + m * TOK, 16), TOK), cols],
            dst.at[pl.ds(pl.multiple_of(dst_off + m * TOK, 16), TOK), cols])
        return cps, own_copy

    def exchange_extra(axis, src_extra, dst_extra):
        m = me[axis]
        cps = []
        for k in (2, 1, 3):
            c = lax.rem(m + k, RING)
            cps.append(remote(src_extra.at[aligned(c, TAIL), :], dst_extra.at[aligned(m, TAIL), :], at(axis, c)))
        dst_extra[aligned(m, TAIL), :] = src_extra[aligned(m, TAIL), :]
        return cps

    def slot_of(ref, c, cols=None):
        rows = pl.ds(pl.multiple_of(c * TOK, 16), TOK)
        return ref.at[rows, :] if cols is None else ref.at[rows, cols]

    LO, HI = pl.ds(0, half), pl.ds(half, half)

    def gather_begin(axis, ref, cols):
        m = me[axis]
        return [remote(slot_of(ref, m, cols), slot_of(ref, m, cols), peer(axis, k))
                for k in ((1, 3) if cols is LO else (3, 1))]

    def gather_relay(axis, ref, low, high):
        m = me[axis]
        before, after = lax.rem(m + 3, RING), lax.rem(m + 1, RING)
        low[0].wait_recv()
        a = remote(slot_of(ref, before, LO), slot_of(ref, before, LO), peer(axis, 1))
        high[0].wait_recv()
        b = remote(slot_of(ref, after, HI), slot_of(ref, after, HI), peer(axis, 3))
        return [a, b, low[1], high[1]]

    def pack_index(f, g, notes):
        wait_recv(notes)
        wide = lax.broadcasted_iota(jnp.int32, (TOK, LANES), 0).astype(F32)
        tail = lax.broadcasted_iota(jnp.int32, (TAIL, LANES), 0)
        tail_place = (TOK + lax.rem(tail, EXTRA)).astype(F32)
        tail_block = tail // EXTRA
        metas = (mo, mp)[g]
        gate = [jnp.zeros((TOK, 1), F32)] * RING
        tail_gate = jnp.zeros((TAIL, 1), F32)
        for q in range(RING):
            m = metas[f, q].astype(F32)
            s = jnp.where(m >= 0, m + q * CAP, -1.0)
            w = m[4:8, :] + m[8:12, :]
            cols = slice(q * LANES, (q + 1) * LANES)
            chosen = jnp.zeros((TAIL, LANES), F32)
            weight = jnp.zeros((TAIL, LANES), F32)
            for t in range(RING):
                row, w_row = s[t : t + 1, :], w[t : t + 1, :]
                hit = wide == row
                oh[t * TOK : (t + 1) * TOK, cols] = jnp.where(hit, 1.0, 0.0).astype(BF16)
                chosen = jnp.where(tail_block == t, row, chosen)
                if f == B:
                    gate[t] += jnp.sum(jnp.where(hit, w_row, 0.0), axis=1, keepdims=True)
                    weight = jnp.where(tail_block == t, w_row, weight)
            hit = chosen == tail_place
            oh[MAIN:ROWS, cols] = jnp.where(hit, 1.0, 0.0).astype(BF16)
            tail_gate += jnp.sum(jnp.where(hit, weight, 0.0), axis=1, keepdims=True)
        if f == B:
            for t in range(RING):
                gc[g, t * TOK : (t + 1) * TOK, :] = jnp.broadcast_to(gate[t], (TOK, LANES))
            gc[g, MAIN:ROWS, :] = jnp.broadcast_to(tail_gate, (TAIL, LANES))

        ix[f, g] = dot(oh[:, 0 : RING * LANES], close[...]).astype(BF16)

    def pack_rows(f, g):
        def cols_step(j, carry):
            cols = aligned(j, 512)
            acc = dot(ix[f, g], G[f][g][0:MAIN, cols])
            if f == B:
                acc = acc * gc[g, :, 0:1]
            PK[f][g][:, cols] = acc.astype(BF16)
            return carry

        lax.fori_loop(0, width // 512, cols_step, 0)
        fold_out(PK[f][g], MAIN, es.at[f, g])

    def weights(f, g):
        lane = lax.broadcasted_iota(jnp.int32, (TOK, ROWS), 1)
        in_main = lane < MAIN
        block = jnp.where(in_main, lane // TOK, (lane - MAIN) // EXTRA)
        place = jnp.where(in_main, lax.rem(lane, TOK), TOK + lax.rem(lane - MAIN, EXTRA)).astype(F32)
        metas = (mo, mp)[g]
        for q in range(RING):
            m = jnp.concatenate([metas[f, q].astype(F32), jnp.zeros((LANES - 16, LANES), F32)], axis=0)
            m = m.T[0:TOK, :]
            s = m[:, 0:1]
            w = m[:, 4:5]
            for t in range(1, RING):
                s = jnp.where(block == t, m[:, t : t + 1], s)
                w = jnp.where(block == t, m[:, 4 + t : 5 + t], w)
            hit = jnp.logical_and(s >= 0, s + q * CAP == place)
            qm[f, g, q * TOK : (q + 1) * TOK, :] = jnp.where(hit, w if f == F else 1.0, 0.0).astype(BF16)

    def combine(f, g, h):
        col0, size = CHUNKS[h]
        fold_in(yr.at[f, g, :, pl.ds(col0 // 4, size // 4)], G[f][g], MAIN, col0, size)

        def cols_step(j, carry):
            cols = aligned(j, 512)
            PK[f][g][0:MAIN, cols] = dot(qm[f, g], G[f][g][:, cols]).astype(BF16)
            return carry

        lax.fori_loop(col0 // 512, (col0 + size) // 512, cols_step, 0)

    def parts(h):
        col0, size = CHUNKS[h]
        return (pl.ds(col0, size // 2), pl.ds(col0 + size // 2, size // 2)), pl.ds(col0 // 2, size // 2), pl.ds(col0, size)

    def scatter_begin(f, g, h):
        axis, ref = AG_AXIS[f][g], PK[f][g]
        (lo, hi), short, _ = parts(h)
        far = lax.rem(me[axis] + 2, RING)
        return [remote(slot_of(ref, far, lo), ra.at[f, g, :, short], peer(axis, 1)),
                remote(slot_of(ref, far, hi), rb.at[f, g, :, short], peer(axis, 3))]

    def scatter_relay(f, g, h, first):
        axis, ref = AG_AXIS[f][g], PK[f][g]
        ends, short, whole = parts(h)
        m = me[axis]
        cps = []
        for i, (k, got, dst) in enumerate(((1, ra, rc), (3, rb, rd))):
            first[i].wait_recv()
            c = lax.rem(m + k, RING)
            rows = pl.ds(pl.multiple_of(c * TOK, 16), TOK)
            ref[rows, ends[i]] = (ref[rows, ends[i]].astype(F32) + got[f, g, :, short].astype(F32)).astype(BF16)
            cps.append(remote(slot_of(ref, c, whole), dst.at[f, g, :, whole], peer(axis, k)))
        return cps

    def scatter_end(f, g, h, cps, out, device):
        axis, ref = AG_AXIS[f][g], PK[f][g]
        col0, size = CHUNKS[h]
        wait_recv(cps)
        rows = pl.ds(pl.multiple_of(me[axis] * TOK, 16), TOK)

        def cols_step(j, carry):
            cols = aligned(j, 512)
            acc = ref[rows, cols].astype(F32) + rc[f, g, :, cols].astype(F32) + rd[f, g, :, cols].astype(F32)
            ref[rows, cols] = acc.astype(BF16)
            return carry

        lax.fori_loop(col0 // 512, (col0 + size) // 512, cols_step, 0)
        whole = pl.ds(col0, size)
        return remote(slot_of(ref, me[axis], whole), out.at[:, whole], device)

    own = [here(tok_hbm, slot_of(g_fo, y)), here(grd_hbm, slot_of(g_bo, x))]
    saved_in = [here(sg_hbm, hb.at[0 : TOK * 8, 0:inner]), here(su_hbm, hb.at[0 : TOK * 8, inner : 2 * inner])]
    begin(wa_pair)
    begin(wd_rows)

    barrier = pltpu.get_barrier_semaphore()
    everyone = [partner, (next_sec, e), (prev_sec, e), (next_sec, other), (prev_sec, other)]
    everyone += [peer(a, k) for a in ("y", "x") for k in (1, 2, 3)]
    for device in everyone:
        pl.semaphore_signal(barrier, inc=1, device_id=device, device_id_type=MESH)
    c = lax.broadcasted_iota(jnp.int32, close.shape, 0)
    j = lax.broadcasted_iota(jnp.int32, close.shape, 1)
    same = jnp.logical_and(c // LANES == j // TOK, lax.rem(c, LANES) == lax.rem(j, TOK))
    close[...] = jnp.where(same, 1.0, 0.0).astype(BF16)
    pl.semaphore_wait(barrier, len(everyone))

    def partner_send(f, cols):
        return remote(
            slot_of(G[f][O], me[AG_AXIS[f][O]], cols), slot_of(G[f][Q], me[AG_AXIS[f][Q]], cols), partner)

    def notes_begin(f):
        axis = AG_AXIS[f][O]
        m = me[axis]
        notes = [remote(meta.at[f, Q], mz.at[f], partner)]
        for k in (1, 2, 3):
            c = lax.rem(m + k, RING)
            notes.append(remote(meta.at[f, O, c], mo.at[f, m], at(axis, c)))
        mo[f, m] = meta[f, O, m]
        return notes

    def partner_notes(f, notes):
        axis = AG_AXIS[f][Q]
        m = me[axis]
        notes[0].wait_recv()
        more = []
        for k in (1, 2, 3):
            c = lax.rem(m + k, RING)
            more.append(remote(mz.at[f, c], mp.at[f, m], at(axis, c)))
        mp[f, m] = mz[f, m]
        return more

    def partner_begin(f, to_z, cols):
        to_z.wait_recv()
        return gather_begin(AG_AXIS[f][Q], G[f][Q], cols)

    def packed(f, g, relays):
        wait_recv(relays)
        pack_rows(f, g)
        return exchange_main(UNI_AXIS[f][g], PK[f][g], 0, X[f], g * ROWS)

    def packed_extra(f, g, sent, relays):
        wait_send(sent + relays[0:2])
        return exchange_extra(UNI_AXIS[f][g], es.at[f, g], er.at[f, g])

    def saved_pack(g, dst):
        index = (lax.broadcasted_iota(jnp.int32, (ROWS, TOK * 8), 0) + g * ROWS).astype(F32)
        oh[...] = jnp.where(spos[0:1, :] == index, 1.0, 0.0).astype(BF16)

        def cols_step(j, carry):
            cols = aligned(j, 512)
            dst[:, cols] = dot(oh[...], hb[0 : TOK * 8, cols]).astype(BF16)
            return carry

        lax.fori_loop(0, 2 * inner // 512, cols_step, 0)
        fold_out(dst, MAIN, spe.at[g])

    own[F].wait()
    of_l = gather_begin("y", g_fo, LO)
    zf_l = partner_send(F, LO)
    of_h = gather_begin("y", g_fo, HI)
    own[B].wait()
    ob_l = gather_begin("x", g_bo, LO)
    zb_l = partner_send(B, LO)
    ob_h = gather_begin("x", g_bo, HI)
    places(F, routes_f, gates_f)
    n_f = notes_begin(F)
    places(B, routes_b, gates_b)
    n_b = notes_begin(B)
    ro_f = gather_relay("y", g_fo, of_l, of_h)
    ro_b = gather_relay("x", g_bo, ob_l, ob_h)
    pf_l = partner_begin(F, zf_l, LO)
    pb_l = partner_begin(B, zb_l, LO)
    zf_h = partner_send(F, HI)
    zb_h = partner_send(B, HI)
    pack_index(F, O, n_f[1:])
    pack_index(B, O, n_b[1:])
    for cp in saved_in:
        cp.wait()
    saved_pack(Q, spk_p)
    uo_f, lo_f = packed(F, O, ro_f)
    uo_b, lo_b = packed(B, O, ro_b)
    pf_h = partner_begin(F, zf_h, HI)
    pb_h = partner_begin(B, zb_h, HI)
    s1_z = [remote(spk_p.at[0:MAIN, :], sz, partner), remote(spe.at[1], sze, partner)]
    np_f = partner_notes(F, n_f)
    np_b = partner_notes(B, n_b)
    uo_f += packed_extra(F, O, [zf_l, zf_h] + of_l + of_h, ro_f)
    uo_b += packed_extra(B, O, [zb_l, zb_h] + ob_l + ob_h, ro_b)
    rp_f = gather_relay("x", g_fp, pf_l, pf_h)
    rp_b = gather_relay("y", g_bp, pb_l, pb_h)
    pack_index(F, Q, np_f)
    pack_index(B, Q, np_b)
    saved_pack(O, spk_o)
    up_f, lp_f = packed(F, Q, rp_f)
    up_f += packed_extra(F, Q, pf_l + pf_h, rp_f)
    s1_o, sl_o = exchange("x", spk_o, 0, spe.at[0], sg_o, 0, sge.at[0])
    up_b, lp_b = packed(B, Q, rp_b)
    up_b += packed_extra(B, Q, pb_l + pb_h, rp_b)
    weights(F, O)
    weights(F, Q)
    wait_recv(s1_z)
    s1_p, sl_p = exchange("y", sz, 0, sze, sg_p, 0, sge.at[1])

    def saved_second(g, first, own_copy, before, got, out):
        wait_recv(first)
        own_copy.wait()
        wait_send(before)
        fold_in(sge.at[g], got, MAIN)

        def cols_step(j, carry):
            cols = aligned(j, 512)
            out[:, cols] = dot(swap[...], got[:, cols]).astype(BF16)
            return carry

        lax.fori_loop(0, 2 * inner // 512, cols_step, 0)
        fold_out(out, MAIN, s2e.at[g])
        return exchange(UNI_AXIS[B][g], out, 0, s2e.at[g], sx, g * ROWS, sxe.at[g])

    weights(B, O)
    weights(B, Q)

    wait_recv(uo_f + up_f)
    lo_f.wait()
    lp_f.wait()
    for g in (O, Q):
        fold_in(er.at[F, g], x_f, g * ROWS + MAIN)

    def fwd_hidden(j, slot):
        for r in range(2):
            rows = slice(r * ROWS, (r + 1) * ROWS)
            both = dot(x_f[rows, :], wa[slot])
            gate, up = both[:, 0:LANES], both[:, LANES : 2 * LANES]
            hb[rows, aligned(j, LANES)] = (gate / (1.0 + jnp.exp(-gate)) * up).astype(BF16)

    stream(inner // LANES, wa_pair, fwd_hidden)
    begin(wa_down)
    s2_o, sm_o = saved_second(O, s1_o, sl_o, s1_o, sg_o, spk_o)
    s2_p, sm_p = saved_second(Q, s1_p, sl_p, s1_z, sg_p, spk_p)

    def fwd_down(j, slot):
        for r in range(2):
            rows = slice(r * ROWS, (r + 1) * ROWS)
            x_f[rows, aligned(j, 256)] = dot(hb[rows, 0:inner], wa[slot, 0:inner, :]).astype(BF16)

    def give_back(f, h):
        col0, size = CHUNKS[h]
        cps, owns = [], []
        for g in (Q, O):
            extra = (f, g, slice(None), pl.ds(col0 // 4, size // 4))
            fold_out(X[f], g * ROWS + MAIN, ys.at[extra], col0, size)
            c, o = exchange(
                UNI_AXIS[f][g], X[f], g * ROWS, ys.at[extra], G[f][g], 0, yr.at[extra], pl.ds(col0, size))
            cps = cps + c
            owns.append(o)
        return cps, owns

    tiles = width // 256
    cut = CHUNKS[0][1] // 256
    stream(tiles, wa_down, fwd_down, 0, cut)
    back_f0 = give_back(F, 0)
    stream(tiles, wa_down, fwd_down, cut, tiles)
    back_f1 = give_back(F, 1)

    wait_recv(uo_b + up_b + s2_o + s2_p)
    for cp in (lo_b, lp_b, sm_o, sm_p):
        cp.wait()
    for g in (O, Q):
        fold_in(er.at[B, g], x_b, g * ROWS + MAIN)
        fold_in(sxe.at[g], sx, g * ROWS + MAIN)

    def bwd_hidden(j, slot):
        cols, more = aligned(j, 256), pl.ds(pl.multiple_of(inner + j * 256, 256), 256)
        for r in range(2):
            rows = slice(r * ROWS, (r + 1) * ROWS)
            grad = dot_t(x_b[rows, :], wd_t[slot])
            a = sx[rows, cols].astype(F32)
            b = sx[rows, more].astype(F32)
            s = 1.0 / (1.0 + jnp.exp(-a))
            hb[rows, cols] = (grad * b * s * (1.0 + a * (1.0 - s))).astype(BF16)
            hb[rows, more] = (grad * a * s).astype(BF16)

    stream(inner // 256, wd_rows, bwd_hidden)
    begin(wd_pair)

    def bwd_down(j, slot):
        for r in range(2):
            rows = slice(r * ROWS, (r + 1) * ROWS)
            x_b[rows, aligned(j, 256)] = dot_t(hb[rows, :], wd_t[slot, :, 0 : 2 * inner]).astype(BF16)

    def sums_begin(f, h, back, before):
        cps, owns = back
        wait_recv(cps)
        for cp in owns:
            cp.wait()
        wait_send(before)
        first = {}
        for g in (Q, O):
            combine(f, g, h)
            first[g] = scatter_begin(f, g, h)
        return first

    def sums_relay(f, h, first):
        return {g: scatter_relay(f, g, h, first[g]) for g in (Q, O)}

    outs = ((out_fo, out_fp), (out_bo, out_bp))
    to_sec = (next_sec, prev_sec)

    def sums_end(f, h, second):
        return [scatter_end(f, g, h, second[g], outs[f][g], (to_sec[f], (e, other)[g])) for g in (Q, O)]

    sent, last = [], []

    def note(cps):
        for g in (Q, O):
            sent.extend(cps[g])
        return cps

    stream(tiles, wd_pair, bwd_down, 0, cut)
    back_b0 = give_back(B, 0)
    stream(tiles, wd_pair, bwd_down, cut, tiles)
    back_b1 = give_back(B, 1)
    f0 = note(sums_begin(F, 0, back_f0, uo_f + up_f))
    f1 = note(sums_begin(F, 1, back_f1, []))
    f0 = note(sums_relay(F, 0, f0))
    b0 = note(sums_begin(B, 0, back_b0, uo_b + up_b))
    f1 = note(sums_relay(F, 1, f1))
    last += sums_end(F, 0, f0)
    b0 = note(sums_relay(B, 0, b0))
    b1 = note(sums_begin(B, 1, back_b1, []))
    last += sums_end(F, 1, f1)
    last += sums_end(B, 0, b0)
    b1 = note(sums_relay(B, 1, b1))
    last += sums_end(B, 1, b1)

    wait_send(sent + back_f0[0] + back_f1[0] + back_b0[0] + back_b1[0])
    wait_send(n_f + np_f + n_b + np_b + s1_p + s2_o + s2_p)
    for cp in last:
        cp.wait()
    assert used[0] <= N_SEMS and used[1] <= N_LOCAL, used


def body(
    fwd_tokens,
    fwd_routes,
    fwd_gates,
    bwd_grads,
    bwd_routes,
    bwd_gates,
    saved_gate,
    saved_up,
    w_gate,
    w_up,
    w_down,
):
    tokens, grads = fwd_tokens[0], bwd_grads[0]
    width, inner = tokens.shape[1], w_gate.shape[3]
    quarter = width // 4
    any_, vmem = pl.BlockSpec(memory_space=pl.ANY), pl.BlockSpec(memory_space=pltpu.VMEM)

    def buf(*shape):
        return pltpu.VMEM(shape, BF16)

    scratch = (
        [buf(ROWS, width)] * 8
        + [buf(2 * ROWS, width)] * 2
        + [buf(2, 2, 4 * TAIL, quarter)] * 4
        + [buf(2, 2, TOK, width // 2)] * 2
        + [buf(2, 2, TOK, width)] * 2
        + [buf(2, TOK, width)]
        + [buf(2, 2, 4, 16, LANES)]
        + [buf(2, 4, 16, LANES)] * 3
        + [pltpu.VMEM((8, LANES), F32), pltpu.VMEM((8, TOK * 8), F32)]
        + [buf(ROWS, 2 * inner)] * 4
        + [buf(MAIN, 2 * inner), buf(2 * ROWS, 2 * inner)]
        + [buf(2, 4 * TAIL, inner // 2)] * 2
        + [buf(4 * TAIL, inner // 2)]
        + [buf(2, 4 * TAIL, inner // 2)] * 2
        + [buf(2 * ROWS, 2 * inner), buf(ROWS, TOK * 8), buf(2, 2, ROWS, MAIN), buf(RING * LANES, MAIN), buf(2, 2, MAIN, ROWS)]
        + [pltpu.VMEM((2, ROWS, LANES), F32)]
        + [buf(2, width, 256), buf(2, 256, width)]
        + [pltpu.SemaphoreType.DMA((N_SEMS,)), pltpu.SemaphoreType.DMA((N_SEMS,))]
        + [pltpu.SemaphoreType.DMA((N_LOCAL,)), pltpu.SemaphoreType.DMA((4, 2))]
    )
    out = jax.ShapeDtypeStruct(tokens.shape, BF16)
    rows = 2 * ROWS
    fo, fp, bo, bp = pl.pallas_call(
        kernel,
        out_shape=(out,) * 4,
        in_specs=[any_] * 7 + [vmem] * 6,
        out_specs=(any_,) * 4,
        scratch_shapes=scratch,
        compiler_params=pltpu.CompilerParams(
            collective_id=1, has_side_effects=True, vmem_limit_bytes=62 * 1024 * 1024
        ),
        cost_estimate=pl.CostEstimate(
            flops=12 * rows * width * inner, bytes_accessed=12 * width * inner, transcendentals=2 * rows * inner
        ),
    )(
        tokens,
        grads,
        saved_gate[0].reshape(-1, inner),
        saved_up[0].reshape(-1, inner),
        w_gate[0, 0],
        w_up[0, 0],
        w_down[0, 0],
        fwd_routes[0].T,
        fwd_gates[0].T,
        bwd_routes[0].T,
        bwd_gates[0].T,
        jnp.asarray(fold_matrix(), BF16),
        jnp.asarray(swap_matrix(), BF16),
    )
    next_inputs = (fo.astype(F32) + fp.astype(F32)).astype(BF16)
    prev_grads = (bo.astype(F32) + bp.astype(F32)).astype(BF16)
    return (next_inputs[None], prev_grads[None])


def solution(mesh):
    return jax.shard_map(
        body,
        mesh=mesh,
        in_specs=(P("section", "expert", None),) * 6 + (P("section", "expert", None, None),) * 5,
        out_specs=(P("section", "expert", None), P("section", "expert", None)),
        check_vma=False,
    )
```

```python
import functools

import jax
import jax.numpy as jnp
import numpy as np
from jax import lax
from jax.experimental import pallas as pl
from jax.experimental.pallas import tpu as pltpu
from jax.sharding import PartitionSpec as P

MESH = pl.DeviceIdType.MESH
F32 = jnp.float32
BF16 = jnp.bfloat16

RING = 4
CAP = 21
TOK = 80
GROUP = RING * CAP
EXTRA = GROUP - TOK
MAIN = RING * TOK
ROWS = RING * GROUP
TAIL = ROWS - MAIN
LANES = 128
N_SEMS = 208
N_LOCAL = 24


def row_of(block, place):
    return block * TOK + place if place < TOK else MAIN + block * EXTRA + place - TOK


def swap_matrix():
    m = np.zeros((ROWS, ROWS), np.float32)
    for q in range(RING):
        for t in range(RING):
            for i in range(CAP):
                m[row_of(t, q * CAP + i), row_of(q, t * CAP + i)] = 1
    return m


def fold_matrix():
    m = np.zeros((4 * TAIL, 4 * TAIL), np.float32)
    for a in range(4):
        for b in range(4):
            for j in range(4):
                m[b * 16 + a * 4 + j, a * 16 + b * 4 + j] = 1
    return m


def dot(a, b):
    return jnp.dot(a, b, preferred_element_type=F32)


def dot_t(a, b):
    return lax.dot_general(a, b, (((1,), (1,)), ((), ())), preferred_element_type=F32)


def aligned(i, size):
    return pl.ds(pl.multiple_of(i * size, size), size)


def kernel(
    tok_hbm,
    grd_hbm,
    sg_hbm,
    su_hbm,
    wg_hbm,
    wu_hbm,
    wd_hbm,
    routes_f, gates_f, routes_b, gates_b,
    fold,
    swap,
    out_fo, out_fp, out_bo, out_bp,
    g_fo, g_fp, g_bo, g_bp,
    pk_fo, pk_fp, pk_bo, pk_bp,
    x_f, x_b,
    es, er, ys, yr,
    ra, rb, rc, rd, zr,
    meta, mo, mz, mp, turn, spos,
    spk_o, spk_p, sg_o, sg_p, sz, sx,
    spe, sge, sze, s2e, sxe,
    hb, oh, ix, close, qm, gc, wa, wd_t,
    send, recv, local, wsem,
):
    e = lax.axis_index("expert")
    sec = lax.axis_index("section")
    n_sec = lax.axis_size("section")
    z, y, x = e // 16, lax.rem(e // 4, 4), lax.rem(e, 4)
    me = {"y": y, "x": x}
    width = tok_hbm.shape[1]
    inner = wg_hbm.shape[1]
    half = width // 2
    F, B, O, Q = 0, 1, 0, 1
    G = ((g_fo, g_fp), (g_bo, g_bp))
    PK = ((pk_fo, pk_fp), (pk_bo, pk_bp))
    X = (x_f, x_b)
    AG_AXIS = (("y", "x"), ("x", "y"))
    UNI_AXIS = (("x", "y"), ("y", "x"))
    CHUNKS = ((0, 2048), (2048, width - 2048))

    def at(axis, c):
        if axis == "y":
            return (sec, z * 16 + c * 4 + x)
        return (sec, z * 16 + y * 4 + c)

    def peer(axis, k):
        return at(axis, lax.rem(me[axis] + k, RING))

    other = (1 - z) * 16 + y * 4 + x
    partner = (sec, other)
    next_sec = lax.rem(sec + 1, n_sec)
    prev_sec = lax.rem(sec + n_sec - 1, n_sec)

    used = [0, 0]

    def remote(src, dst, device):
        i = used[0]
        used[0] += 1
        cp = pltpu.make_async_remote_copy(
            src_ref=src, dst_ref=dst, send_sem=send.at[i], recv_sem=recv.at[i],
            device_id=device, device_id_type=MESH,
        )
        cp.start()
        return cp

    def here(src, dst):
        i = used[1]
        used[1] += 1
        cp = pltpu.make_async_copy(src, dst, local.at[i])
        cp.start()
        return cp

    def wait_recv(cps):
        for cp in cps:
            cp.wait_recv()

    def wait_send(cps):
        for cp in cps:
            cp.wait_send()

    def turned(ref, fill):
        turn[...] = jnp.full((8, LANES), fill, F32)
        turn[:, 0:TOK] = ref[...].astype(F32)
        return turn[...]

    def places(f, routes, gates):
        named_by = turned(routes, -1.0)
        gate_by = turned(gates, 0.0)
        expert = lax.broadcasted_iota(jnp.int32, (32, LANES), 0).astype(F32)
        hot = [named_by[k : k + 1, :] == expert for k in range(8)]
        count = jnp.zeros((32, LANES), F32)
        gate = jnp.zeros((32, LANES), F32)
        for k in range(8):
            count += jnp.where(hot[k], 1.0, 0.0)
            gate += jnp.where(hot[k], gate_by[k : k + 1, :], 0.0)
        earlier = lax.broadcasted_iota(jnp.int32, (LANES, LANES), 0) < lax.broadcasted_iota(jnp.int32, (LANES, LANES), 1)
        within = dot(count.astype(BF16), jnp.where(earlier, 1.0, 0.0).astype(BF16))
        high = gate.astype(BF16).astype(F32)
        rows = jnp.concatenate([jnp.where(count > 0, within, -1.0), high, gate - high], axis=0).astype(BF16)
        r = lax.broadcasted_iota(jnp.int32, (64, 96), 0)
        message, kind, item = r // 16, lax.rem(r, 16) // 4, lax.rem(r, 4)
        col = lax.broadcasted_iota(jnp.int32, (64, 96), 1)
        for g in (O, Q):
            plane = z if g == O else 1 - z
            if AG_AXIS[f][g] == "y":
                index = plane * 16 + message * 4 + item
            else:
                index = plane * 16 + item * 4 + message
            pick = jnp.where(jnp.logical_and(kind < 3, col == kind * 32 + index), 1.0, 0.0).astype(BF16)
            got = dot(pick, rows).astype(BF16)
            for c in range(4):
                meta[f, g, c] = got[c * 16 : (c + 1) * 16, :]
        if f == F:
            return
        slot = jnp.concatenate(
            [jnp.sum(jnp.where(hot[k], within, 0.0), axis=0, keepdims=True) for k in range(8)], axis=0
        ).astype(jnp.int32)
        chosen = named_by.astype(jnp.int32)
        same = chosen // 16 == z
        cy, cx = lax.rem(chosen // 4, 4), lax.rem(chosen, 4)
        block = jnp.where(same, cx, cy)
        place = jnp.where(same, cy, cx) * CAP + slot
        row = jnp.where(place < TOK, block * TOK + place, MAIN + block * EXTRA + place - TOK)
        row = row + jnp.where(same, 0, ROWS)
        token = lax.broadcasted_iota(jnp.int32, (LANES, TOK * 8), 0)
        lane = lax.broadcasted_iota(jnp.int32, (LANES, TOK * 8), 1)
        spread = jnp.where(lane // 8 == token, 1.0, 0.0).astype(BF16)
        coarse = (row // 16).astype(F32).astype(BF16)
        fine = lax.rem(row, 16).astype(F32).astype(BF16)
        wide = 16.0 * dot(coarse, spread) + dot(fine, spread)
        mine = lax.broadcasted_iota(jnp.int32, (8, TOK * 8), 0) == lax.rem(lane[0:8, :], 8)
        total = jnp.sum(jnp.where(mine, wide, 0.0), axis=0, keepdims=True)
        spos[...] = jnp.broadcast_to(total, (8, TOK * 8))

    def wa_pair(j, slot):
        cols = pl.ds(pl.multiple_of(j * LANES, LANES), LANES)
        return (
            pltpu.make_async_copy(wg_hbm.at[:, cols], wa.at[slot, :, 0:LANES], wsem.at[0, slot]),
            pltpu.make_async_copy(wu_hbm.at[:, cols], wa.at[slot, :, LANES : 2 * LANES], wsem.at[1, slot]),
        )

    def wa_down(j, slot):
        cols = pl.ds(pl.multiple_of(j * 256, 256), 256)
        return (pltpu.make_async_copy(wd_hbm.at[:, cols], wa.at[slot, 0:inner, :], wsem.at[0, slot]),)

    def wd_rows(j, slot):
        rows = aligned(j, 256)
        return (pltpu.make_async_copy(wd_hbm.at[rows, :], wd_t.at[slot], wsem.at[2, slot]),)

    def wd_pair(j, slot):
        rows = aligned(j, 256)
        return (
            pltpu.make_async_copy(wg_hbm.at[rows, :], wd_t.at[slot, :, 0:inner], wsem.at[2, slot]),
            pltpu.make_async_copy(wu_hbm.at[rows, :], wd_t.at[slot, :, inner : 2 * inner], wsem.at[3, slot]),
        )

    def begin(tiles):
        for cp in tiles(0, 0):
            cp.start()

    def stream(n, tiles, work, first=0, last=None):
        def step(j, carry):
            slot = lax.rem(j, 2)

            @pl.when(j + 1 < n)
            def _():
                for cp in tiles(j + 1, 1 - slot):
                    cp.start()

            for cp in tiles(j, slot):
                cp.wait()
            work(j, slot)
            return carry

        lax.fori_loop(first, n if last is None else last, step, 0)

    def fold_out(src, row0, dst, col0=0, size=None):
        w4 = (src.shape[1] if size is None else size) // 4
        a = jnp.concatenate(
            [src[row0 : row0 + TAIL, col0 + c * w4 : col0 + (c + 1) * w4] for c in range(4)], axis=0)
        dst[...] = dot(fold[...], a).astype(BF16)

    def fold_in(src, dst, row0, col0=0, size=None):
        w4 = (dst.shape[1] if size is None else size) // 4
        a = dot(fold[...], src[...]).astype(BF16)
        for c in range(4):
            dst[row0 : row0 + TAIL, col0 + c * w4 : col0 + (c + 1) * w4] = a[c * TAIL : (c + 1) * TAIL, :]

    def exchange(axis, src, src_off, src_extra, dst, dst_off, dst_extra, cols=slice(None)):
        cps, own_copy = exchange_main(axis, src, src_off, dst, dst_off, cols)
        return cps + exchange_extra(axis, src_extra, dst_extra), own_copy

    def exchange_main(axis, src, src_off, dst, dst_off, cols=slice(None)):
        m = me[axis]
        cps = []
        for k in (2, 1, 3):
            c = lax.rem(m + k, RING)
            cps.append(remote(
                src.at[pl.ds(pl.multiple_of(src_off + c * TOK, 16), TOK), cols],
                dst.at[pl.ds(pl.multiple_of(dst_off + m * TOK, 16), TOK), cols],
                at(axis, c)))
        own_copy = here(
            src.at[pl.ds(pl.multiple_of(src_off + m * TOK, 16), TOK), cols],
            dst.at[pl.ds(pl.multiple_of(dst_off + m * TOK, 16), TOK), cols])
        return cps, own_copy

    def exchange_extra(axis, src_extra, dst_extra):
        m = me[axis]
        cps = []
        for k in (2, 1, 3):
            c = lax.rem(m + k, RING)
            cps.append(remote(src_extra.at[aligned(c, TAIL), :], dst_extra.at[aligned(m, TAIL), :], at(axis, c)))
        dst_extra[aligned(m, TAIL), :] = src_extra[aligned(m, TAIL), :]
        return cps

    def slot_of(ref, c, cols=None):
        rows = pl.ds(pl.multiple_of(c * TOK, 16), TOK)
        return ref.at[rows, :] if cols is None else ref.at[rows, cols]

    LO, HI = pl.ds(0, half), pl.ds(half, half)

    def gather_begin(axis, ref, cols):
        m = me[axis]
        return [remote(slot_of(ref, m, cols), slot_of(ref, m, cols), peer(axis, k))
                for k in ((1, 3) if cols is LO else (3, 1))]

    def gather_relay(axis, ref, low, high):
        m = me[axis]
        before, after = lax.rem(m + 3, RING), lax.rem(m + 1, RING)
        low[0].wait_recv()
        a = remote(slot_of(ref, before, LO), slot_of(ref, before, LO), peer(axis, 1))
        high[0].wait_recv()
        b = remote(slot_of(ref, after, HI), slot_of(ref, after, HI), peer(axis, 3))
        return [a, b, low[1], high[1]]

    def pack_index(f, g, notes):
        wait_recv(notes)
        wide = lax.broadcasted_iota(jnp.int32, (TOK, LANES), 0).astype(F32)
        tail = lax.broadcasted_iota(jnp.int32, (TAIL, LANES), 0)
        tail_place = (TOK + lax.rem(tail, EXTRA)).astype(F32)
        tail_block = tail // EXTRA
        metas = (mo, mp)[g]
        gate = [jnp.zeros((TOK, 1), F32)] * RING
        tail_gate = jnp.zeros((TAIL, 1), F32)
        for q in range(RING):
            m = metas[f, q].astype(F32)
            s = jnp.where(m >= 0, m + q * CAP, -1.0)
            w = m[4:8, :] + m[8:12, :]
            cols = slice(q * LANES, (q + 1) * LANES)
            chosen = jnp.zeros((TAIL, LANES), F32)
            weight = jnp.zeros((TAIL, LANES), F32)
            for t in range(RING):
                row, w_row = s[t : t + 1, :], w[t : t + 1, :]
                hit = wide == row
                oh[t * TOK : (t + 1) * TOK, cols] = jnp.where(hit, 1.0, 0.0).astype(BF16)
                chosen = jnp.where(tail_block == t, row, chosen)
                if f == B:
                    gate[t] += jnp.sum(jnp.where(hit, w_row, 0.0), axis=1, keepdims=True)
                    weight = jnp.where(tail_block == t, w_row, weight)
            hit = chosen == tail_place
            oh[MAIN:ROWS, cols] = jnp.where(hit, 1.0, 0.0).astype(BF16)
            tail_gate += jnp.sum(jnp.where(hit, weight, 0.0), axis=1, keepdims=True)
        if f == B:
            for t in range(RING):
                gc[g, t * TOK : (t + 1) * TOK, :] = jnp.broadcast_to(gate[t], (TOK, LANES))
            gc[g, MAIN:ROWS, :] = jnp.broadcast_to(tail_gate, (TAIL, LANES))

        ix[f, g] = dot(oh[:, 0 : RING * LANES], close[...]).astype(BF16)

    def pack_rows(f, g):
        def cols_step(j, carry):
            cols = aligned(j, 512)
            acc = dot(ix[f, g], G[f][g][0:MAIN, cols])
            if f == B:
                acc = acc * gc[g, :, 0:1]
            PK[f][g][:, cols] = acc.astype(BF16)
            return carry

        lax.fori_loop(0, width // 512, cols_step, 0)
        fold_out(PK[f][g], MAIN, es.at[f, g])

    def weights(f, g):
        lane = lax.broadcasted_iota(jnp.int32, (TOK, ROWS), 1)
        in_main = lane < MAIN
        block = jnp.where(in_main, lane // TOK, (lane - MAIN) // EXTRA)
        place = jnp.where(in_main, lax.rem(lane, TOK), TOK + lax.rem(lane - MAIN, EXTRA)).astype(F32)
        metas = (mo, mp)[g]
        for q in range(RING):
            m = jnp.concatenate([metas[f, q].astype(F32), jnp.zeros((LANES - 16, LANES), F32)], axis=0)
            m = m.T[0:TOK, :]
            s = m[:, 0:1]
            w = m[:, 4:5]
            for t in range(1, RING):
                s = jnp.where(block == t, m[:, t : t + 1], s)
                w = jnp.where(block == t, m[:, 4 + t : 5 + t], w)
            hit = jnp.logical_and(s >= 0, s + q * CAP == place)
            qm[f, g, q * TOK : (q + 1) * TOK, :] = jnp.where(hit, w if f == F else 1.0, 0.0).astype(BF16)

    def combine(f, g, h):
        col0, size = CHUNKS[h]
        fold_in(yr.at[f, g, :, pl.ds(col0 // 4, size // 4)], G[f][g], MAIN, col0, size)

        def cols_step(j, carry):
            cols = aligned(j, 512)
            PK[f][g][0:MAIN, cols] = dot(qm[f, g], G[f][g][:, cols]).astype(BF16)
            return carry

        lax.fori_loop(col0 // 512, (col0 + size) // 512, cols_step, 0)

    def parts(h):
        col0, size = CHUNKS[h]
        return (pl.ds(col0, size // 2), pl.ds(col0 + size // 2, size // 2)), pl.ds(col0 // 2, size // 2), pl.ds(col0, size)

    direct = {}

    def scatter_begin(f, g, h):
        axis, ref = AG_AXIS[f][g], PK[f][g]
        (lo, hi), short, _ = parts(h)
        far = lax.rem(me[axis] + 2, RING)
        first = [remote(slot_of(ref, far, lo), ra.at[f, g, :, short], peer(axis, 1)),
                 remote(slot_of(ref, far, hi), rb.at[f, g, :, short], peer(axis, 3))]
        direct[f, g, h] = [
            remote(slot_of(ref, lax.rem(me[axis] + k, RING), cols), dst.at[f, g, :, cols], peer(axis, k))
            for k, cols, dst in ((1, hi, rc), (3, lo, rd))]
        return first + direct[f, g, h]

    def scatter_relay(f, g, h, first):
        axis, ref = AG_AXIS[f][g], PK[f][g]
        ends, short, _ = parts(h)
        m = me[axis]
        cps = []
        for i, (k, got, dst) in enumerate(((1, ra, rc), (3, rb, rd))):
            first[i].wait_recv()
            c = lax.rem(m + k, RING)
            rows = pl.ds(pl.multiple_of(c * TOK, 16), TOK)
            ref[rows, ends[i]] = (ref[rows, ends[i]].astype(F32) + got[f, g, :, short].astype(F32)).astype(BF16)
            cps.append(remote(slot_of(ref, c, ends[i]), dst.at[f, g, :, ends[i]], peer(axis, k)))
        return cps

    def scatter_end(f, g, h, cps, out, device):
        axis, ref = AG_AXIS[f][g], PK[f][g]
        col0, size = CHUNKS[h]
        wait_recv(cps + direct[f, g, h])
        rows = pl.ds(pl.multiple_of(me[axis] * TOK, 16), TOK)

        def cols_step(j, carry):
            cols = aligned(j, 512)
            acc = ref[rows, cols].astype(F32) + rc[f, g, :, cols].astype(F32) + rd[f, g, :, cols].astype(F32)
            ref[rows, cols] = acc.astype(BF16)
            return carry

        lax.fori_loop(col0 // 512, (col0 + size) // 512, cols_step, 0)
        whole = pl.ds(col0, size)
        return remote(slot_of(ref, me[axis], whole), out.at[:, whole], device)

    own = [here(tok_hbm, slot_of(g_fo, y)), here(grd_hbm, slot_of(g_bo, x))]
    saved_in = [here(sg_hbm, hb.at[0 : TOK * 8, 0:inner]), here(su_hbm, hb.at[0 : TOK * 8, inner : 2 * inner])]
    begin(wa_pair)
    begin(wd_rows)

    barrier = pltpu.get_barrier_semaphore()
    everyone = [partner, (next_sec, e), (prev_sec, e), (next_sec, other), (prev_sec, other)]
    everyone += [peer(a, k) for a in ("y", "x") for k in (1, 2, 3)]
    for device in everyone:
        pl.semaphore_signal(barrier, inc=1, device_id=device, device_id_type=MESH)
    c = lax.broadcasted_iota(jnp.int32, close.shape, 0)
    j = lax.broadcasted_iota(jnp.int32, close.shape, 1)
    same = jnp.logical_and(c // LANES == j // TOK, lax.rem(c, LANES) == lax.rem(j, TOK))
    close[...] = jnp.where(same, 1.0, 0.0).astype(BF16)
    pl.semaphore_wait(barrier, len(everyone))

    def partner_send(f, cols):
        return remote(
            slot_of(G[f][O], me[AG_AXIS[f][O]], cols), slot_of(G[f][Q], me[AG_AXIS[f][Q]], cols), partner)

    def notes_begin(f):
        axis = AG_AXIS[f][O]
        m = me[axis]
        notes = [remote(meta.at[f, Q], mz.at[f], partner)]
        for k in (1, 2, 3):
            c = lax.rem(m + k, RING)
            notes.append(remote(meta.at[f, O, c], mo.at[f, m], at(axis, c)))
        mo[f, m] = meta[f, O, m]
        return notes

    def partner_notes(f, notes):
        axis = AG_AXIS[f][Q]
        m = me[axis]
        notes[0].wait_recv()
        more = []
        for k in (1, 2, 3):
            c = lax.rem(m + k, RING)
            more.append(remote(mz.at[f, c], mp.at[f, m], at(axis, c)))
        mp[f, m] = mz[f, m]
        return more

    def partner_begin(f, to_z, cols):
        to_z.wait_recv()
        return gather_begin(AG_AXIS[f][Q], G[f][Q], cols)

    def packed(f, g, relays):
        wait_recv(relays)
        pack_rows(f, g)
        return exchange_main(UNI_AXIS[f][g], PK[f][g], 0, X[f], g * ROWS)

    def packed_extra(f, g, sent, relays):
        wait_send(sent + relays[0:2])
        return exchange_extra(UNI_AXIS[f][g], es.at[f, g], er.at[f, g])

    def saved_pack(g, dst):
        index = (lax.broadcasted_iota(jnp.int32, (ROWS, TOK * 8), 0) + g * ROWS).astype(F32)
        oh[...] = jnp.where(spos[0:1, :] == index, 1.0, 0.0).astype(BF16)

        def cols_step(j, carry):
            cols = aligned(j, 512)
            dst[:, cols] = dot(oh[...], hb[0 : TOK * 8, cols]).astype(BF16)
            return carry

        lax.fori_loop(0, 2 * inner // 512, cols_step, 0)
        fold_out(dst, MAIN, spe.at[g])

    own[F].wait()
    of_l = gather_begin("y", g_fo, LO)
    zf_l = partner_send(F, LO)
    of_h = gather_begin("y", g_fo, HI)
    own[B].wait()
    ob_l = gather_begin("x", g_bo, LO)
    zb_l = partner_send(B, LO)
    ob_h = gather_begin("x", g_bo, HI)
    places(F, routes_f, gates_f)
    n_f = notes_begin(F)
    places(B, routes_b, gates_b)
    n_b = notes_begin(B)
    ro_f = gather_relay("y", g_fo, of_l, of_h)
    ro_b = gather_relay("x", g_bo, ob_l, ob_h)
    pf_l = partner_begin(F, zf_l, LO)
    pb_l = partner_begin(B, zb_l, LO)
    zf_h = partner_send(F, HI)
    zb_h = partner_send(B, HI)
    pack_index(F, O, n_f[1:])
    pack_index(B, O, n_b[1:])
    for cp in saved_in:
        cp.wait()
    saved_pack(Q, spk_p)
    uo_f, lo_f = packed(F, O, ro_f)
    uo_b, lo_b = packed(B, O, ro_b)
    pf_h = partner_begin(F, zf_h, HI)
    pb_h = partner_begin(B, zb_h, HI)
    s1_z = [remote(spk_p.at[0:MAIN, :], sz, partner), remote(spe.at[1], sze, partner)]
    np_f = partner_notes(F, n_f)
    np_b = partner_notes(B, n_b)
    uo_f += packed_extra(F, O, [zf_l, zf_h] + of_l + of_h, ro_f)
    uo_b += packed_extra(B, O, [zb_l, zb_h] + ob_l + ob_h, ro_b)
    rp_f = gather_relay("x", g_fp, pf_l, pf_h)
    rp_b = gather_relay("y", g_bp, pb_l, pb_h)
    pack_index(F, Q, np_f)
    pack_index(B, Q, np_b)
    saved_pack(O, spk_o)
    up_f, lp_f = packed(F, Q, rp_f)
    up_f += packed_extra(F, Q, pf_l + pf_h, rp_f)
    s1_o, sl_o = exchange("x", spk_o, 0, spe.at[0], sg_o, 0, sge.at[0])
    up_b, lp_b = packed(B, Q, rp_b)
    up_b += packed_extra(B, Q, pb_l + pb_h, rp_b)
    weights(F, O)
    weights(F, Q)
    wait_recv(s1_z)
    s1_p, sl_p = exchange("y", sz, 0, sze, sg_p, 0, sge.at[1])

    def saved_second(g, first, own_copy, before, got, out):
        wait_recv(first)
        own_copy.wait()
        wait_send(before)
        fold_in(sge.at[g], got, MAIN)

        def cols_step(j, carry):
            cols = aligned(j, 512)
            out[:, cols] = dot(swap[...], got[:, cols]).astype(BF16)
            return carry

        lax.fori_loop(0, 2 * inner // 512, cols_step, 0)
        fold_out(out, MAIN, s2e.at[g])
        return exchange(UNI_AXIS[B][g], out, 0, s2e.at[g], sx, g * ROWS, sxe.at[g])

    weights(B, O)
    weights(B, Q)

    wait_recv(uo_f + up_f)
    lo_f.wait()
    lp_f.wait()
    for g in (O, Q):
        fold_in(er.at[F, g], x_f, g * ROWS + MAIN)

    def fwd_hidden(j, slot):
        for r in range(2):
            rows = slice(r * ROWS, (r + 1) * ROWS)
            both = dot(x_f[rows, :], wa[slot])
            gate, up = both[:, 0:LANES], both[:, LANES : 2 * LANES]
            hb[rows, aligned(j, LANES)] = (gate / (1.0 + jnp.exp(-gate)) * up).astype(BF16)

    stream(inner // LANES, wa_pair, fwd_hidden)
    begin(wa_down)
    s2_o, sm_o = saved_second(O, s1_o, sl_o, s1_o, sg_o, spk_o)
    s2_p, sm_p = saved_second(Q, s1_p, sl_p, s1_z, sg_p, spk_p)

    def fwd_down(j, slot):
        for r in range(2):
            rows = slice(r * ROWS, (r + 1) * ROWS)
            x_f[rows, aligned(j, 256)] = dot(hb[rows, 0:inner], wa[slot, 0:inner, :]).astype(BF16)

    def give_back(f, h):
        col0, size = CHUNKS[h]
        cps, owns = [], []
        for g in (Q, O):
            extra = (f, g, slice(None), pl.ds(col0 // 4, size // 4))
            fold_out(X[f], g * ROWS + MAIN, ys.at[extra], col0, size)
            c, o = exchange(
                UNI_AXIS[f][g], X[f], g * ROWS, ys.at[extra], G[f][g], 0, yr.at[extra], pl.ds(col0, size))
            cps = cps + c
            owns.append(o)
        return cps, owns

    tiles = width // 256
    cut = CHUNKS[0][1] // 256
    stream(tiles, wa_down, fwd_down, 0, cut)
    back_f0 = give_back(F, 0)
    stream(tiles, wa_down, fwd_down, cut, tiles)
    back_f1 = give_back(F, 1)

    wait_recv(uo_b + up_b + s2_o + s2_p)
    for cp in (lo_b, lp_b, sm_o, sm_p):
        cp.wait()
    for g in (O, Q):
        fold_in(er.at[B, g], x_b, g * ROWS + MAIN)
        fold_in(sxe.at[g], sx, g * ROWS + MAIN)

    def bwd_hidden(j, slot):
        cols, more = aligned(j, 256), pl.ds(pl.multiple_of(inner + j * 256, 256), 256)
        for r in range(2):
            rows = slice(r * ROWS, (r + 1) * ROWS)
            grad = dot_t(x_b[rows, :], wd_t[slot])
            a = sx[rows, cols].astype(F32)
            b = sx[rows, more].astype(F32)
            s = 1.0 / (1.0 + jnp.exp(-a))
            hb[rows, cols] = (grad * b * s * (1.0 + a * (1.0 - s))).astype(BF16)
            hb[rows, more] = (grad * a * s).astype(BF16)

    stream(inner // 256, wd_rows, bwd_hidden)
    begin(wd_pair)

    def bwd_down(j, slot):
        for r in range(2):
            rows = slice(r * ROWS, (r + 1) * ROWS)
            x_b[rows, aligned(j, 256)] = dot_t(hb[rows, :], wd_t[slot, :, 0 : 2 * inner]).astype(BF16)

    def sums_begin(f, h, back, before):
        cps, owns = back
        wait_recv(cps)
        for cp in owns:
            cp.wait()
        wait_send(before)
        first = {}
        for g in (Q, O):
            combine(f, g, h)
            first[g] = scatter_begin(f, g, h)
        return first

    def sums_relay(f, h, first):
        return {g: scatter_relay(f, g, h, first[g]) for g in (Q, O)}

    outs = ((out_fo, out_fp), (out_bo, out_bp))
    to_sec = (next_sec, prev_sec)

    def sums_end(f, h, second):
        return [scatter_end(f, g, h, second[g], outs[f][g], (to_sec[f], (e, other)[g])) for g in (Q, O)]

    sent, last = [], []

    def note(cps):
        for g in (Q, O):
            sent.extend(cps[g])
        return cps

    stream(tiles, wd_pair, bwd_down, 0, cut)
    back_b0 = give_back(B, 0)
    stream(tiles, wd_pair, bwd_down, cut, tiles)
    back_b1 = give_back(B, 1)
    f0 = note(sums_begin(F, 0, back_f0, uo_f + up_f))
    f1 = note(sums_begin(F, 1, back_f1, []))
    f0 = note(sums_relay(F, 0, f0))
    b0 = note(sums_begin(B, 0, back_b0, uo_b + up_b))
    f1 = note(sums_relay(F, 1, f1))
    last += sums_end(F, 0, f0)
    b0 = note(sums_relay(B, 0, b0))
    b1 = note(sums_begin(B, 1, back_b1, []))
    last += sums_end(F, 1, f1)
    last += sums_end(B, 0, b0)
    b1 = note(sums_relay(B, 1, b1))
    last += sums_end(B, 1, b1)

    wait_send(sent + back_f0[0] + back_f1[0] + back_b0[0] + back_b1[0])
    wait_send(n_f + np_f + n_b + np_b + s1_p + s2_o + s2_p)
    for cp in last:
        cp.wait()
    assert used[0] <= N_SEMS and used[1] <= N_LOCAL, used


def body(
    fwd_tokens,
    fwd_routes,
    fwd_gates,
    bwd_grads,
    bwd_routes,
    bwd_gates,
    saved_gate,
    saved_up,
    w_gate,
    w_up,
    w_down,
):
    tokens, grads = fwd_tokens[0], bwd_grads[0]
    width, inner = tokens.shape[1], w_gate.shape[3]
    quarter = width // 4
    any_, vmem = pl.BlockSpec(memory_space=pl.ANY), pl.BlockSpec(memory_space=pltpu.VMEM)

    def buf(*shape):
        return pltpu.VMEM(shape, BF16)

    scratch = (
        [buf(ROWS, width)] * 8
        + [buf(2 * ROWS, width)] * 2
        + [buf(2, 2, 4 * TAIL, quarter)] * 4
        + [buf(2, 2, TOK, width // 2)] * 2
        + [buf(2, 2, TOK, width)] * 2
        + [buf(2, TOK, width)]
        + [buf(2, 2, 4, 16, LANES)]
        + [buf(2, 4, 16, LANES)] * 3
        + [pltpu.VMEM((8, LANES), F32), pltpu.VMEM((8, TOK * 8), F32)]
        + [buf(ROWS, 2 * inner)] * 4
        + [buf(MAIN, 2 * inner), buf(2 * ROWS, 2 * inner)]
        + [buf(2, 4 * TAIL, inner // 2)] * 2
        + [buf(4 * TAIL, inner // 2)]
        + [buf(2, 4 * TAIL, inner // 2)] * 2
        + [buf(2 * ROWS, 2 * inner), buf(ROWS, TOK * 8), buf(2, 2, ROWS, MAIN), buf(RING * LANES, MAIN), buf(2, 2, MAIN, ROWS)]
        + [pltpu.VMEM((2, ROWS, LANES), F32)]
        + [buf(2, width, 256), buf(2, 256, width)]
        + [pltpu.SemaphoreType.DMA((N_SEMS,)), pltpu.SemaphoreType.DMA((N_SEMS,))]
        + [pltpu.SemaphoreType.DMA((N_LOCAL,)), pltpu.SemaphoreType.DMA((4, 2))]
    )
    out = jax.ShapeDtypeStruct(tokens.shape, BF16)
    rows = 2 * ROWS
    fo, fp, bo, bp = pl.pallas_call(
        kernel,
        out_shape=(out,) * 4,
        in_specs=[any_] * 7 + [vmem] * 6,
        out_specs=(any_,) * 4,
        scratch_shapes=scratch,
        compiler_params=pltpu.CompilerParams(
            collective_id=1, has_side_effects=True, vmem_limit_bytes=62 * 1024 * 1024
        ),
        cost_estimate=pl.CostEstimate(
            flops=12 * rows * width * inner, bytes_accessed=12 * width * inner, transcendentals=2 * rows * inner
        ),
    )(
        tokens,
        grads,
        saved_gate[0].reshape(-1, inner),
        saved_up[0].reshape(-1, inner),
        w_gate[0, 0],
        w_up[0, 0],
        w_down[0, 0],
        fwd_routes[0].T,
        fwd_gates[0].T,
        bwd_routes[0].T,
        bwd_gates[0].T,
        jnp.asarray(fold_matrix(), BF16),
        jnp.asarray(swap_matrix(), BF16),
    )
    next_inputs = (fo.astype(F32) + fp.astype(F32)).astype(BF16)
    prev_grads = (bo.astype(F32) + bp.astype(F32)).astype(BF16)
    return (next_inputs[None], prev_grads[None])


def solution(mesh):
    return jax.shard_map(
        body,
        mesh=mesh,
        in_specs=(P("section", "expert", None),) * 6 + (P("section", "expert", None, None),) * 5,
        out_specs=(P("section", "expert", None), P("section", "expert", None)),
        check_vma=False,
    )
```
